256 devices in a mesh: dp: 8 (over x, core), expert: 32 (over y, z).
Axes of the slice: x: 4, y: 4, z: 8, core: 2. Of those that a mesh axis runs over, the one named last changes fastest.
Arguments:
- tokens: bfloat16 [32768, 3072], P(('dp', 'expert')), may hold values from -6 to 6
- routes: int32 [32768, 2], P(('dp', 'expert')), may hold values from 0 to 31, as said below
- router_gates: int32 [32768, 2], P(('dp', 'expert')), may hold values from 1024 to 32767
- hidden_cotangent: bfloat16 [32768, 2, 768], P(('dp', 'expert')), may hold values from -6 to 6
- weights: bfloat16 [2, 32, 768, 3072], P(None, None, 'expert', 'dp'), may hold values from -0.109375 to 0.109375
- first_moment: bfloat16 [2, 32, 768, 3072], P(None, None, 'expert', 'dp'), may hold values from -6 to 6
- second_moment: bfloat16 [2, 32, 768, 3072], P(None, None, 'expert', 'dp'), may hold values from 0.5 to 4
Outputs:
- token_grads: bfloat16 [32768, 3072], P(('dp', 'expert'))
- new_weights: bfloat16 [2, 32, 768, 3072], P(None, 'expert', None, 'dp')
- new_first: bfloat16 [2, 32, 768, 3072], P(None, 'expert', None, 'dp')
- new_second: bfloat16 [2, 32, 768, 3072], P(None, 'expert', None, 'dp')
The draws below stay inside these ranges and needn't reach their ends.
Inputs may be any that keep to these rules, and one draw needn't show every extreme that they name: `routes`: each row names 2 different experts; the rows of one device name any one expert at most 12 times.
All inputs are finite; a program needn't handle non-finite values.
Results may differ from the reference program's by a relative error of at most 0.0075.
Values may be sent and summed in bfloat16 or wider, within the bound.
A program may use at most 128 MiB of HBM per device.

```python
import math
import jax
import jax.numpy as jnp
from jax import lax

D = 3072
H = 768
TOP = 2
TOK = 128
E = 32
CAP = 12
TOKENS = 32768
N_DP = 8
N_EXPERT = 32


def draw_routes(key, part):
    key = jax.random.fold_in(key, 11)
    blocks = TOKENS // TOK
    hot_key, order_key, place_key, shift_key, other_key = jax.random.split(key, 5)
    hot_expert = jax.random.randint(hot_key, (), 0, E)
    orders = jax.vmap(lambda item: jax.random.permutation(item, TOK))(jax.random.split(order_key, blocks))
    is_hot = orders < CAP
    hot_place = jax.random.randint(place_key, (blocks, TOK), 0, TOP)
    needed = jnp.where(is_hot, TOP - 1, TOP)
    starts = jnp.cumsum(needed, axis=1) - needed
    shifts = jax.random.randint(shift_key, (blocks, 1), 0, E - 1)
    others = jax.vmap(lambda item: jax.random.permutation(item, E - 1))(jax.random.split(other_key, blocks))
    others = others + (others >= hot_expert).astype(jnp.int32)
    columns = []
    for column in range(TOP):
        offset = jnp.where(is_hot & (column > hot_place), column - 1, column)
        counter = (starts + offset + shifts) % (E - 1)
        picked = jnp.take_along_axis(others, counter, axis=1)
        columns.append(jnp.where(is_hot & (column == hot_place), hot_expert, picked))
    return jnp.stack(columns, axis=-1).reshape(TOKENS, TOP).astype(jnp.int32)


def set_ends(drawn, key, low, top_value):
    spot = [jax.random.randint(jax.random.fold_in(key, axis), (), 0, length) for axis, length in enumerate(drawn.shape)]
    main_axis = drawn.shape.index(max(drawn.shape))
    beside = spot[:main_axis] + [(spot[main_axis] + 1) % drawn.shape[main_axis]] + spot[main_axis + 1:]
    return drawn.at[tuple(spot)].set(low).at[tuple(beside)].set(top_value)


def level_of(rng, extent, pieces, low, largest):
    gain, own = 1.0, jax.random.fold_in(rng, 6)
    for dim, parts in pieces:
        steps = jnp.exp(jax.random.uniform(jax.random.fold_in(own, dim), (parts,), jnp.float32, low / len(pieces), largest / len(pieces)))
        gain = gain * jnp.repeat(steps, extent[dim] // parts).reshape([-1 if axis == dim else 1 for axis in range(len(extent))])
    return gain


def noise(stream_key, extent, width, reach, cuts=(), held_as=jnp.bfloat16):
    factor_of = level_of(stream_key, extent, cuts, -0.22, 0.18) if cuts else 1.0
    result = jax.random.normal(stream_key, extent, jnp.float32) * width * factor_of
    return jnp.minimum(jnp.maximum(result, -reach), reach).astype(held_as)


def setup_inputs(seed: int = 0) -> dict:
    arg_keys = jax.random.split(jax.random.key(seed), 8)
    return {
        "tokens": noise(arg_keys[0], (TOKENS, D), 1.0, 6.0, ((0, 256),)),
        "routes": draw_routes(jax.random.fold_in(arg_keys[7], 71), 0),
        "router_gates": set_ends(jax.random.randint(arg_keys[2], (TOKENS, TOP), 1024, 32768), jax.random.fold_in(arg_keys[2], 1), 1024, 32767).astype(jnp.int32),
        "hidden_cotangent": noise(arg_keys[3], (TOKENS, TOP, H), 1.0, 6.0, ((0, 256),)),
        "weights": noise(arg_keys[4], (2, E, H, D), D ** -0.5, 0.109375, ((2, 32), (3, 8))),
        "first_moment": noise(arg_keys[5], (2, E, H, D), 1.0, 6.0, ((2, 32), (3, 8))),
        "second_moment": jnp.clip(jnp.exp(math.log(4.0) - 2.0794415 * jax.random.uniform(arg_keys[6], (2, E, H, D), jnp.float32) ** level_of(arg_keys[6], (2, E, H, D), ((2, 32), (3, 8)), -0.2, 0.2)), 0.5, 4.0).astype(jnp.bfloat16),
    }


gate_unit = 32768.0
loss_scale = 16.0
beta_one = 0.9
beta_two = 0.95
step_size = 0.001
adam_eps = 1e-08

def swiglu_backward(slot_rows, upstream, pair_weights):
    pair_float = pair_weights.astype(jnp.float32)
    projected = jnp.einsum('rd,ahd->rah', slot_rows.astype(jnp.float32), pair_float)
    pre_gate = projected[:, 0]
    pre_up = projected[:, 1]
    sigmoid_gate = jax.nn.sigmoid(pre_gate)
    upstream_float = upstream.astype(jnp.float32)
    grad_up = (upstream_float * pre_gate * sigmoid_gate).astype(jnp.bfloat16)
    grad_gate = (upstream_float * pre_up * sigmoid_gate * (1.0 + pre_gate * (1.0 - sigmoid_gate))).astype(jnp.bfloat16)
    paired = jnp.stack([grad_gate, grad_up], axis=1)
    backward = jnp.einsum('rah,ahd->rd', paired.astype(jnp.float32), pair_float).astype(jnp.bfloat16)
    return (backward, paired)

def reference(tokens, routes, router_gates, hidden_cotangent, weights, first_moment, second_moment):
    token_total = tokens.shape[0]
    model_width = tokens.shape[1]
    experts = weights.shape[1]
    hidden_units = weights.shape[2]
    blocks = token_total // TOK
    slot_count = N_EXPERT * CAP
    routings = token_total * TOP
    flat_route = routes.reshape(blocks, TOK * TOP)
    onehot = (flat_route[:, :, None] == jnp.arange(experts, dtype=jnp.int32)[None, None, :]).astype(jnp.int32)
    position = lax.optimization_barrier(jnp.sum((jnp.cumsum(onehot, axis=1) - onehot) * onehot, axis=2))
    block_ids = jnp.arange(blocks, dtype=jnp.int32)
    source = block_ids % N_EXPERT
    group_of = block_ids // N_EXPERT
    target = (group_of[:, None] * experts + flat_route) * slot_count + source[:, None] * CAP + position
    routing_ids = jnp.arange(routings, dtype=jnp.int32)
    slot_table = jnp.full((N_DP * experts * slot_count,), routings, jnp.int32)
    slot_table = slot_table.at[target.reshape(-1)].set(routing_ids).reshape(N_DP, experts, slot_count)
    gate_factor = router_gates.astype(jnp.float32) / gate_unit
    scaled = (gate_factor[:, :, None] * hidden_cotangent.astype(jnp.float32)).astype(jnp.bfloat16)
    scaled = scaled.reshape(routings, hidden_units)

    def per_expert(routed, expert_index):
        pair_weights = lax.dynamic_index_in_dim(weights, expert_index, 1, keepdims=False)

        def per_group(carried, group_index):
            routed_all, grad_total = carried
            slot_ids = slot_table[group_index, expert_index]
            filled = slot_ids < routings
            token_index = jnp.where(filled, slot_ids // TOP, 0).astype(jnp.int32)
            slot_rows = jnp.where(filled[:, None], tokens[token_index], jnp.zeros((), jnp.bfloat16))
            upstream = jnp.where(filled[:, None], scaled[jnp.minimum(slot_ids, routings - 1)], jnp.zeros((), jnp.bfloat16))
            backward, paired = swiglu_backward(slot_rows, upstream, pair_weights)
            partial_sum = jnp.einsum('rah,rd->ahd', paired.astype(jnp.float32), slot_rows.astype(jnp.float32))
            rounded = lax.optimization_barrier(partial_sum.astype(jnp.bfloat16)).astype(jnp.float32)
            routed_all = routed_all.at[slot_ids].set(backward, mode='drop')
            return ((routed_all, grad_total + rounded), None)
        start_sum = jnp.zeros((2, hidden_units, model_width), jnp.float32)
        (routed, grad_total), _ = lax.scan(per_group, (routed, start_sum), jnp.arange(N_DP, dtype=jnp.int32))
        gradient = grad_total / loss_scale
        first_old = lax.dynamic_index_in_dim(first_moment, expert_index, 1, keepdims=False).astype(jnp.float32)
        second_old = lax.dynamic_index_in_dim(second_moment, expert_index, 1, keepdims=False).astype(jnp.float32)
        moment_one = beta_one * first_old + (1.0 - beta_one) * gradient
        moment_two = beta_two * second_old + (1.0 - beta_two) * gradient * gradient
        updated = pair_weights.astype(jnp.float32) - step_size * moment_one / (jnp.sqrt(moment_two) + adam_eps)
        return (routed, (updated.astype(jnp.bfloat16), moment_one.astype(jnp.bfloat16), moment_two.astype(jnp.bfloat16)))
    start_routed = jnp.zeros((routings, model_width), jnp.bfloat16)
    routed, results = lax.scan(per_expert, start_routed, jnp.arange(experts, dtype=jnp.int32))
    new_weights = jnp.swapaxes(results[0], 0, 1)
    new_first = jnp.swapaxes(results[1], 0, 1)
    new_second = jnp.swapaxes(results[2], 0, 1)
    token_grads = lax.optimization_barrier(jnp.sum(routed.reshape(token_total, TOP, model_width).astype(jnp.float32), axis=1)).astype(jnp.bfloat16)
    return (token_grads, new_weights, new_first, new_second)
```

```python
import functools

import jax
import jax.numpy as jnp
import numpy as np
from jax import lax
from jax.experimental import pallas as pl
from jax.experimental.pallas import tpu as pltpu
from jax.sharding import PartitionSpec as P

gate_unit = 32768.0
loss_scale = 16.0
beta_one = 0.9
beta_two = 0.95
step_size = 0.001
adam_eps = 1e-08

MESH = pl.DeviceIdType.MESH
F32 = jnp.float32
BF16 = jnp.bfloat16
CORES = 2
QUARTERS = 4
HALVES = 2
GROUP = 4
W, ROWS, COTS, M1, M2, BACK = range(6)


def dot(a, b, dims=((1,), (0,))):
    return lax.dot_general(a, b, (dims, ((), ())), preferred_element_type=F32)


def kernel(
    nx,
    ny,
    nz,
    cap,
    routes_row,
    routes_col,
    tokens,
    scaled,
    swap,
    fold,
    w,
    m1,
    m2,
    token_out,
    w_out,
    m1_out,
    m2_out,
    rows_s,
    rows_r,
    cots_s,
    cots_r,
    w_r,
    m1_r,
    m2_r,
    full_w,
    x_mat,
    cot_mat,
    pair,
    pair_t,
    back_r,
    grads,
    half_r,
    quarter_r,
    send,
    recv,
    gather_send,
    gather_recv,
    twin_send,
    twin_recv,
    half_send,
    half_recv,
    sum_send,
    sum_recv,
):
    n = ny * nz
    dp, me = lax.axis_index("dp"), lax.axis_index("expert")
    x, core = dp // CORES, dp % CORES
    y, z = me // nz, me % nz
    twin = x * CORES + 1 - core
    tok, width = tokens.shape
    hidden = scaled.shape[1] // 2
    quarter, half = width // QUARTERS, hidden // HALVES
    per_source, cols = w.shape[2], w.shape[3]
    block = QUARTERS * cap
    cot_block = HALVES * cap
    groups = n // GROUP
    span = GROUP * cap
    slots = n * cap

    def peer(i):
        return lax.rem(y + i // nz, ny) * nz + lax.rem(z + i % nz, nz)

    def x_peer(d):
        return lax.rem(x + d, nx) * CORES + core

    barrier = pltpu.get_barrier_semaphore()

    def greet(i, _):
        pl.semaphore_signal(barrier, inc=1, device_id=(dp, peer(i)), device_id_type=MESH)
        return 0

    lax.fori_loop(1, n, greet, 0)
    for d in range(1, nx):
        pl.semaphore_signal(barrier, inc=1, device_id=(x_peer(d), me), device_id_type=MESH)
    pl.semaphore_signal(barrier, inc=1, device_id=(twin, me), device_id_type=MESH)
    pl.semaphore_wait(barrier, n - 1 + nx - 1 + 1)

    def spread(kind, source, landing):
        def start(i, _):
            to = peer(i)
            pltpu.make_async_remote_copy(
                src_ref=source(to),
                dst_ref=landing(me),
                send_sem=send.at[kind],
                recv_sem=recv.at[kind],
                device_id=(dp, to),
                device_id_type=MESH,
            ).start()
            return 0

        lax.fori_loop(1, n, start, 0)
        pltpu.make_async_copy(source(me), landing(me), recv.at[kind]).start()

    def arrived(kind, ref):
        pltpu.make_async_copy(ref, ref, recv.at[kind]).wait()

    def left(kind, ref):
        pltpu.make_async_copy(ref, ref, send.at[kind]).wait()

    spread(W, lambda e: w.at[:, e], lambda s: w_r.at[:, s])

    experts = n
    earlier = lax.broadcasted_iota(jnp.int32, (tok, tok), 0)
    later = lax.broadcasted_iota(jnp.int32, (tok, tok), 1)
    ids = lax.broadcasted_iota(jnp.int32, (experts, tok), 0)
    route_rows = [routes_row[k : k + 1, :] for k in range(2)]
    hot = [(ids == r).astype(F32) for r in route_rows]
    before = dot((hot[0] + hot[1]).astype(BF16), (earlier < later).astype(BF16))
    pos_row = [jnp.sum(h * before, axis=0, keepdims=True).astype(jnp.int32) for h in hot]

    piece = lax.broadcasted_iota(jnp.int32, (GROUP * block, tok), 0)
    cot_piece = lax.broadcasted_iota(jnp.int32, (GROUP * cot_block, tok), 0)

    def pack(g, _):
        first = g * (GROUP * block)
        total = jnp.zeros((GROUP * block, quarter), F32)
        for q in range(QUARTERS):
            spot = [r * block + p + q * cap - first for r, p in zip(route_rows, pos_row)]
            pick = (piece == spot[0]) | (piece == spot[1])
            total += dot(pick.astype(BF16), tokens[:, q * quarter : (q + 1) * quarter])
        rows_s[pl.ds(g * GROUP, GROUP)] = total.astype(BF16).reshape(GROUP, block, quarter)
        first = g * (GROUP * cot_block)
        total = jnp.zeros((GROUP * cot_block, half), F32)
        for k in range(2):
            for h in range(HALVES):
                spot = route_rows[k] * cot_block + pos_row[k] + h * cap - first
                pick = (cot_piece == spot).astype(BF16)
                start = k * hidden + h * half
                total += dot(pick, scaled[:, start : start + half])
        cots_s[pl.ds(g * GROUP, GROUP)] = total.reshape(GROUP, cot_block, half).astype(BF16)
        return 0

    lax.fori_loop(0, groups, pack, 0)

    left(W, w_r.at[:, pl.ds(0, n - 1)])
    spread(COTS, lambda e: cots_s.at[e], lambda s: cots_r.at[s])
    spread(ROWS, lambda e: rows_s.at[e], lambda s: rows_r.at[s])

    arrived(W, w_r)

    def own_columns(i, _):
        for a in range(2):
            part = w_r[a, pl.ds(i * GROUP, GROUP)].astype(F32)
            rows = GROUP * per_source
            full_w[dp, pl.ds(a * hidden + i * rows, rows), :] = part.reshape(rows, cols).astype(BF16)
        return 0

    lax.fori_loop(0, groups, own_columns, 0)

    def gather(d):
        return pltpu.make_async_remote_copy(
            src_ref=full_w.at[dp],
            dst_ref=full_w.at[dp],
            send_sem=gather_send.at[d - 1],
            recv_sem=gather_recv.at[d - 1],
            device_id=(x_peer(d), me),
            device_id_type=MESH,
        )

    def hand_over(d):
        held = lax.rem(x - d + nx, nx) * CORES + core
        return pltpu.make_async_remote_copy(
            src_ref=full_w.at[held],
            dst_ref=full_w.at[held],
            send_sem=twin_send.at[d],
            recv_sem=twin_recv.at[d],
            device_id=(twin, me),
            device_id_type=MESH,
        )

    for d in range(1, nx):
        gather(d).start()
    hand_over(0).start()
    for d in range(1, nx):
        gather(d).wait_recv()
        hand_over(d).start()

    arrived(COTS, cots_r)

    def order_cots(g, _):
        part = cots_r[pl.ds(g * GROUP, GROUP)].astype(F32).reshape(GROUP * cot_block, half)
        part = dot(fold[...], part.astype(BF16)).astype(BF16)
        for h in range(HALVES):
            cot_mat[pl.ds(g * span, span), h * half : (h + 1) * half] = part[h * span : (h + 1) * span]
        return 0

    lax.fori_loop(0, groups, order_cots, 0)
    arrived(ROWS, rows_r)
    spread(M1, lambda e: m1.at[:, e], lambda s: m1_r.at[:, s])
    spread(M2, lambda e: m2.at[:, e], lambda s: m2_r.at[:, s])

    def order_rows(g, _):
        part = rows_r[pl.ds(g * GROUP, GROUP)].reshape(GROUP * block, quarter)
        part = dot(swap[...], part).astype(BF16)
        for q in range(QUARTERS):
            x_mat[pl.ds(g * span, span), q * quarter : (q + 1) * quarter] = part[q * span : (q + 1) * span]
        return 0

    lax.fori_loop(0, groups, order_rows, 0)

    for d in range(nx):
        hand_over(d).wait_recv()

    tile = min(256, hidden)
    for t in range(hidden // tile):
        at = t * tile
        gate_w = jnp.concatenate([full_w[j, at : at + tile] for j in range(nx * CORES)], axis=1)
        pre_gate = dot(x_mat[...], gate_w, ((1,), (1,)))
        at += hidden
        up_w = jnp.concatenate([full_w[j, at : at + tile] for j in range(nx * CORES)], axis=1)
        pre_up = dot(x_mat[...], up_w, ((1,), (1,)))
        at -= hidden
        s = jax.nn.sigmoid(pre_gate)
        upstream = cot_mat[:, at : at + tile].astype(F32)
        grad_up = upstream * pre_gate * s
        grad_gate = upstream * pre_up * s * (1.0 + pre_gate * (1.0 - s))
        pair[:, at : at + tile] = grad_gate.astype(BF16)
        pair[:, hidden + at : hidden + at + tile] = grad_up.astype(BF16)
        pair_t[at : at + tile, :] = grad_gate.T.astype(BF16)
        pair_t[hidden + at : hidden + at + tile, :] = grad_up.T.astype(BF16)

    per_quarter = nx * CORES // QUARTERS
    for q in range(QUARTERS):
        parts = [dot(pair[...], full_w[q * per_quarter + i]) for i in range(per_quarter)]
        part = jnp.concatenate(parts, axis=1).astype(BF16)
        for g in range(groups):
            rows_r[g * GROUP + q] = part[g * span : (g + 1) * span]

    left(COTS, cots_s.at[pl.ds(0, n - 1)])
    left(ROWS, rows_s.at[pl.ds(0, n - 1)])

    def order_back(g, _):
        part = rows_r[pl.ds(g * GROUP, GROUP)].reshape(GROUP * block, quarter)
        part = dot(swap[...], part).astype(BF16)
        rows_s[pl.ds(g * GROUP, GROUP)] = part.reshape(GROUP, block, quarter)
        return 0

    lax.fori_loop(0, groups, order_back, 0)
    spread(BACK, lambda e: rows_s.at[e], lambda s: back_r.at[s])

    chunk = min(384, 2 * hidden)

    def weight_grad(j):
        at = pl.multiple_of(j * cols, cols)

        def rows_of(r, _):
            spot = pl.ds(pl.multiple_of(r * chunk, chunk), chunk)
            grads[j, spot, :] = dot(pair_t[spot, :], x_mat[:, pl.ds(at, cols)]).astype(BF16)
            return 0

        lax.fori_loop(0, 2 * hidden // chunk, rows_of, 0)

    def halve(d):
        return pltpu.make_async_remote_copy(
            src_ref=grads.at[lax.rem(x + d, nx) * CORES + 1 - core],
            dst_ref=half_r.at[d - 1],
            send_sem=half_send.at[d - 1],
            recv_sem=half_recv.at[d - 1],
            device_id=(twin, me),
            device_id_type=MESH,
        )

    def pass_on(d):
        return pltpu.make_async_remote_copy(
            src_ref=grads.at[x_peer(d)],
            dst_ref=quarter_r.at[d - 1],
            send_sem=sum_send.at[d - 1],
            recv_sem=sum_recv.at[d - 1],
            device_id=(x_peer(d), me),
            device_id_type=MESH,
        )

    for d in range(1, nx + 1):
        weight_grad(lax.rem(x + d, nx) * CORES + 1 - core)
        halve(d).start()
    for d in range(1, nx + 1):
        weight_grad(x_peer(d))
        halve(d).wait_recv()
        if d < nx:

            def add(r, _):
                spot = pl.ds(pl.multiple_of(r * chunk, chunk), chunk)
                both = grads[x_peer(d), spot, :].astype(F32) + half_r[d - 1, spot, :].astype(F32)
                grads[x_peer(d), spot, :] = both.astype(BF16)
                return 0

            lax.fori_loop(0, 2 * hidden // chunk, add, 0)
            pass_on(d).start()

    for d in range(1, nx):
        pass_on(d).wait_recv()
    arrived(M1, m1_r)
    arrived(M2, m2_r)

    rows = GROUP * per_source

    def adam(i, _):
        for a in range(2):
            spot = pl.ds(a * hidden + i * rows, rows)
            total = grads[dp, spot, :].astype(F32) + half_r[nx - 1, spot, :].astype(F32)
            for d in range(nx - 1):
                total += quarter_r[d, spot, :].astype(F32)
            gradient = total * (1.0 / loss_scale)
            first = m1_r[a, pl.ds(i * GROUP, GROUP)].astype(F32).reshape(rows, cols)
            second = m2_r[a, pl.ds(i * GROUP, GROUP)].astype(F32).reshape(rows, cols)
            first = beta_one * first + (1.0 - beta_one) * gradient
            second = beta_two * second + (1.0 - beta_two) * gradient * gradient
            weight = full_w[dp, spot, :].astype(F32)
            weight = weight - step_size * first / (jnp.sqrt(second) + adam_eps)
            out = pl.ds(i * rows, rows)
            w_out[a, out, :] = weight.astype(BF16)
            m1_out[a, out, :] = first.astype(BF16)
            m2_out[a, out, :] = second.astype(BF16)
        return 0

    lax.fori_loop(0, groups, adam, 0)

    ids = lax.broadcasted_iota(jnp.int32, (tok, experts), 1)
    route_cols = [routes_col[:, k : k + 1] for k in range(2)]
    hot = [(ids == r).astype(F32) for r in route_cols]
    before = dot((earlier > later).astype(BF16), (hot[0] + hot[1]).astype(BF16))
    spots = [
        r * block + jnp.sum(h * before, axis=1, keepdims=True).astype(jnp.int32)
        for r, h in zip(route_cols, hot)
    ]
    piece = lax.broadcasted_iota(jnp.int32, (tok, n * block), 1)

    arrived(BACK, back_r)
    returned = back_r[...].reshape(n * block, quarter)
    for q in range(QUARTERS):
        pick = (piece == spots[0] + q * cap) | (piece == spots[1] + q * cap)
        token_out[:, q * quarter : (q + 1) * quarter] = dot(pick.astype(BF16), returned).astype(BF16)

    for d in range(1, nx):
        gather(d).wait_send()
        pass_on(d).wait_send()
    for d in range(nx):
        hand_over(d).wait_send()
        halve(d + 1).wait_send()
    left(M1, m1_r.at[:, pl.ds(0, n - 1)])
    left(M2, m2_r.at[:, pl.ds(0, n - 1)])
    left(BACK, rows_s.at[pl.ds(0, n - 1)])


def swap_matrix(outer, inner, cap):
    size = outer * inner * cap
    order = np.arange(size).reshape(inner, outer, cap).transpose(1, 0, 2).reshape(-1)
    matrix = np.zeros((size, size), np.float32)
    matrix[np.arange(size), order] = 1.0
    return jnp.asarray(matrix, BF16)


def per_device(
    mesh_sizes, tokens, routes, router_gates, hidden_cotangent, weights, first_moment, second_moment
):
    ndp, n = mesh_sizes
    nx = ndp // CORES
    nz = min(8, n)
    ny = n // nz
    tok, width = tokens.shape
    hidden = hidden_cotangent.shape[2]
    cap = 3 * tok * 2 // (2 * n)
    per_source, cols = weights.shape[2], weights.shape[3]
    gate_factor = router_gates.astype(F32) / gate_unit
    scaled = (gate_factor[:, :, None] * hidden_cotangent.astype(F32)).astype(BF16)
    scaled = scaled.reshape(tok, 2 * hidden)
    block, cot_block, slots = QUARTERS * cap, HALVES * cap, n * cap
    vmem = pl.BlockSpec(memory_space=pltpu.VMEM)
    hbm = pl.BlockSpec(memory_space=pl.ANY)
    state = jax.ShapeDtypeStruct((2, hidden, cols), BF16)
    dma = pltpu.SemaphoreType.DMA
    token_grads, new_w, new_first, new_second = pl.pallas_call(
        functools.partial(kernel, nx, ny, nz, cap),
        out_shape=(jax.ShapeDtypeStruct((tok, width), BF16), state, state, state),
        in_specs=[vmem] * 6 + [hbm] * 3,
        out_specs=(vmem,) * 4,
        scratch_shapes=[
            pltpu.VMEM((n, block, width // QUARTERS), BF16),
            pltpu.VMEM((n, block, width // QUARTERS), BF16),
            pltpu.VMEM((n, cot_block, hidden // HALVES), BF16),
            pltpu.VMEM((n, cot_block, hidden // HALVES), BF16),
            pltpu.VMEM((2, n, per_source, cols), BF16),
            pltpu.VMEM((2, n, per_source, cols), BF16),
            pltpu.VMEM((2, n, per_source, cols), BF16),
            pltpu.VMEM((ndp, 2 * hidden, cols), BF16),
            pltpu.VMEM((slots, width), BF16),
            pltpu.VMEM((slots, hidden), BF16),
            pltpu.VMEM((slots, 2 * hidden), BF16),
            pltpu.VMEM((2 * hidden, slots), BF16),
            pltpu.VMEM((n, block, width // QUARTERS), BF16),
            pltpu.VMEM((ndp, 2 * hidden, cols), BF16),
            pltpu.VMEM((nx, 2 * hidden, cols), BF16),
            pltpu.VMEM((nx - 1, 2 * hidden, cols), BF16),
            dma((6,)),
            dma((6,)),
            dma((nx - 1,)),
            dma((nx - 1,)),
            dma((nx,)),
            dma((nx,)),
            dma((nx,)),
            dma((nx,)),
            dma((nx - 1,)),
            dma((nx - 1,)),
        ],
        compiler_params=pltpu.CompilerParams(
            collective_id=0, has_side_effects=True, vmem_limit_bytes=60 * 1024 * 1024
        ),
        name="experts_step",
    )(
        routes.T,
        routes,
        tokens,
        scaled,
        swap_matrix(QUARTERS, GROUP, cap),
        swap_matrix(HALVES, GROUP, cap),
        weights,
        first_moment,
        second_moment,
    )
    shape = (2, 1, hidden, cols)
    return token_grads, new_w.reshape(shape), new_first.reshape(shape), new_second.reshape(shape)


def solution(mesh):
    placed = (
        P(("dp", "expert"), None),
        P(("dp", "expert"), None),
        P(("dp", "expert"), None),
        P(("dp", "expert"), None, None),
        P(None, None, "expert", "dp"),
        P(None, None, "expert", "dp"),
        P(None, None, "expert", "dp"),
    )
    return jax.shard_map(
        functools.partial(per_device, (mesh.shape["dp"], mesh.shape["expert"])),
        mesh=mesh,
        in_specs=placed,
        out_specs=(
            P(("dp", "expert"), None),
            P(None, "expert", None, "dp"),
            P(None, "expert", None, "dp"),
            P(None, "expert", None, "dp"),
        ),
        check_vma=False,
    )
```

```python
import functools

import jax
import jax.numpy as jnp
from jax import lax
from jax.experimental import pallas as pl
from jax.experimental.pallas import tpu as pltpu
from jax.sharding import PartitionSpec as P

gate_unit = 32768.0
loss_scale = 16.0
beta_one = 0.9
beta_two = 0.95
step_size = 0.001
adam_eps = 1e-08

MESH = pl.DeviceIdType.MESH
F32 = jnp.float32
BF16 = jnp.bfloat16
CORES = 2
QUARTERS = 4
HALVES = 2
GROUP = 4
W, ROWS, COTS, M1, M2, BACK = range(6)


def dot(a, b, dims=((1,), (0,))):
    return lax.dot_general(a, b, (dims, ((), ())), preferred_element_type=F32)


def order_matrix(outer, inner, cap):
    size = outer * inner * cap
    row = lax.broadcasted_iota(jnp.int32, (size, size), 0)
    source = lax.broadcasted_iota(jnp.int32, (size, size), 1)
    a = sum((row >= i * inner * cap).astype(jnp.int32) for i in range(1, outer))
    rest = row - a * (inner * cap)
    b = sum((rest >= i * cap).astype(jnp.int32) for i in range(1, inner))
    return (source == b * (outer * cap) + a * cap + rest - b * cap).astype(BF16)


def kernel(
    nx,
    ny,
    nz,
    cap,
    routes,
    gates,
    tokens,
    cotangent,
    w,
    m1,
    m2,
    token_out,
    w_out,
    m1_out,
    m2_out,
    rows_s,
    rows_r,
    cots_s,
    cots_r,
    scaled,
    w_r,
    m1_r,
    m2_r,
    full_w,
    x_mat,
    cot_mat,
    pair,
    pair_t,
    back_r,
    grads,
    half_r,
    quarter_r,
    swap,
    fold,
    send,
    recv,
    gather_send,
    gather_recv,
    twin_send,
    twin_recv,
    half_send,
    half_recv,
    sum_send,
    sum_recv,
):
    n = ny * nz
    dp, me = lax.axis_index("dp"), lax.axis_index("expert")
    x, core = dp // CORES, dp % CORES
    y, z = me // nz, me % nz
    twin = x * CORES + 1 - core
    tok, width = tokens.shape
    hidden = cotangent.shape[2]
    quarter, half = width // QUARTERS, hidden // HALVES
    per_source, cols = w.shape[2], w.shape[3]
    block = QUARTERS * cap
    cot_block = HALVES * cap
    groups = n // GROUP
    span = GROUP * cap
    slots = n * cap

    def peer(i):
        step = i // ny
        dz = jnp.where(step % 2 == 1, (step + 1) // 2, nz - step // 2)
        return lax.rem(y + i % ny, ny) * nz + lax.rem(z + dz, nz)

    def x_peer(d):
        return lax.rem(x + d, nx) * CORES + core

    barrier = pltpu.get_barrier_semaphore()

    def greet(i, _):
        pl.semaphore_signal(barrier, inc=1, device_id=(dp, peer(i)), device_id_type=MESH)
        return 0

    lax.fori_loop(1, n, greet, 0)
    for d in range(1, nx):
        pl.semaphore_signal(barrier, inc=1, device_id=(x_peer(d), me), device_id_type=MESH)
    pl.semaphore_signal(barrier, inc=1, device_id=(twin, me), device_id_type=MESH)
    pl.semaphore_wait(barrier, n - 1 + nx - 1 + 1)

    def spread(kind, source, landing, parts=((ny, n), (1, ny))):
        def start(i, _):
            to = peer(i)
            pltpu.make_async_remote_copy(
                src_ref=source(to),
                dst_ref=landing(me),
                send_sem=send.at[kind],
                recv_sem=recv.at[kind],
                device_id=(dp, to),
                device_id_type=MESH,
            ).start()
            return 0

        for first, last in parts:
            lax.fori_loop(first, last, start, 0)
        pltpu.make_async_copy(source(me), landing(me), recv.at[kind]).start()

    def arrived(kind, ref):
        pltpu.make_async_copy(ref, ref, recv.at[kind]).wait()

    def left(kind, ref):
        pltpu.make_async_copy(ref, ref, send.at[kind]).wait()

    spread(W, lambda e: w.at[:, e], lambda s: w_r.at[:, s])

    experts = n
    earlier = lax.broadcasted_iota(jnp.int32, (tok, tok), 0)
    later = lax.broadcasted_iota(jnp.int32, (tok, tok), 1)
    ids = lax.broadcasted_iota(jnp.int32, (experts, tok), 0)
    route_rows = [routes[k : k + 1, :] for k in range(2)]
    hot = [(ids == r).astype(F32) for r in route_rows]
    before = dot((hot[0] + hot[1]).astype(BF16), (earlier < later).astype(BF16))
    pos_row = [jnp.sum(h * before, axis=0, keepdims=True).astype(jnp.int32) for h in hot]

    def column(row):
        return jnp.sum(jnp.where(earlier == later, row, jnp.zeros_like(row)), axis=1, keepdims=True)

    spots = [column(r * block + p) for r, p in zip(route_rows, pos_row)]
    for k in range(2):
        factor = column(gates[k : k + 1, :].astype(F32)) * (1.0 / gate_unit)
        scaled[:, k * hidden : (k + 1) * hidden] = (factor * cotangent[:, k, :].astype(F32)).astype(BF16)

    swap[...] = order_matrix(QUARTERS, GROUP, cap)
    fold[...] = order_matrix(HALVES, GROUP, cap)

    piece = lax.broadcasted_iota(jnp.int32, (GROUP * block, tok), 0)
    cot_piece = lax.broadcasted_iota(jnp.int32, (GROUP * cot_block, tok), 0)

    def pack_cots(g, _):
        first = g * (GROUP * cot_block)
        total = jnp.zeros((GROUP * cot_block, half), F32)
        for k in range(2):
            for h in range(HALVES):
                spot = route_rows[k] * cot_block + pos_row[k] + h * cap - first
                pick = (cot_piece == spot).astype(BF16)
                start = k * hidden + h * half
                total += dot(pick, scaled[:, start : start + half])
        cots_s[pl.ds(g * GROUP, GROUP)] = total.reshape(GROUP, cot_block, half).astype(BF16)
        return 0

    def pack_rows(g, _):
        first = g * (GROUP * block)
        total = jnp.zeros((GROUP * block, quarter), F32)
        for q in range(QUARTERS):
            spot = [r * block + p + q * cap - first for r, p in zip(route_rows, pos_row)]
            pick = (piece == spot[0]) | (piece == spot[1])
            total += dot(pick.astype(BF16), tokens[:, q * quarter : (q + 1) * quarter])
        rows_s[pl.ds(g * GROUP, GROUP)] = total.astype(BF16).reshape(GROUP, block, quarter)
        return 0

    lax.fori_loop(0, groups, pack_cots, 0)
    spread(COTS, lambda e: cots_s.at[e], lambda s: cots_r.at[s])
    lax.fori_loop(0, groups, pack_rows, 0)

    left(W, w_r.at[:, pl.ds(0, n - 1)])
    spread(ROWS, lambda e: rows_s.at[e], lambda s: rows_r.at[s])

    arrived(W, w_r)

    def own_columns(i, _):
        for a in range(2):
            part = w_r[a, pl.ds(i * GROUP, GROUP)].astype(F32)
            rows = GROUP * per_source
            full_w[dp, pl.ds(a * hidden + i * rows, rows), :] = part.reshape(rows, cols).astype(BF16)
        return 0

    lax.fori_loop(0, groups, own_columns, 0)

    def gather(d):
        return pltpu.make_async_remote_copy(
            src_ref=full_w.at[dp],
            dst_ref=full_w.at[dp],
            send_sem=gather_send.at[d - 1],
            recv_sem=gather_recv.at[d - 1],
            device_id=(x_peer(d), me),
            device_id_type=MESH,
        )

    def hand_over(d):
        held = lax.rem(x - d + nx, nx) * CORES + core
        return pltpu.make_async_remote_copy(
            src_ref=full_w.at[held],
            dst_ref=full_w.at[held],
            send_sem=twin_send.at[d],
            recv_sem=twin_recv.at[d],
            device_id=(twin, me),
            device_id_type=MESH,
        )

    for d in range(1, nx):
        gather(d).start()
    hand_over(0).start()
    for d in range(1, nx):
        gather(d).wait_recv()
        hand_over(d).start()

    arrived(COTS, cots_r)

    def order_cots(g, _):
        part = cots_r[pl.ds(g * GROUP, GROUP)].astype(F32).reshape(GROUP * cot_block, half)
        part = dot(fold[...], part.astype(BF16)).astype(BF16)
        for h in range(HALVES):
            cot_mat[pl.ds(g * span, span), h * half : (h + 1) * half] = part[h * span : (h + 1) * span]
        return 0

    lax.fori_loop(0, groups, order_cots, 0)
    left(COTS, cots_s.at[pl.ds(0, n - 1)])
    left(ROWS, rows_s.at[pl.ds(0, n - 1)])
    spread(M1, lambda e: m1.at[:, e], lambda s: m1_r.at[:, s])
    spread(M2, lambda e: m2.at[:, e], lambda s: m2_r.at[:, s])
    arrived(ROWS, rows_r)

    def order_rows(g, _):
        part = rows_r[pl.ds(g * GROUP, GROUP)].reshape(GROUP * block, quarter)
        part = dot(swap[...], part).astype(BF16)
        for q in range(QUARTERS):
            x_mat[pl.ds(g * span, span), q * quarter : (q + 1) * quarter] = part[q * span : (q + 1) * span]
        return 0

    lax.fori_loop(0, groups, order_rows, 0)

    for d in range(nx):
        hand_over(d).wait_recv()

    tile = min(256, hidden)
    for t in range(hidden // tile):
        at = t * tile
        gate_w = jnp.concatenate([full_w[j, at : at + tile] for j in range(nx * CORES)], axis=1)
        pre_gate = dot(x_mat[...], gate_w, ((1,), (1,)))
        at += hidden
        up_w = jnp.concatenate([full_w[j, at : at + tile] for j in range(nx * CORES)], axis=1)
        pre_up = dot(x_mat[...], up_w, ((1,), (1,)))
        at -= hidden
        s = jax.nn.sigmoid(pre_gate)
        upstream = cot_mat[:, at : at + tile].astype(F32)
        grad_up = upstream * pre_gate * s
        grad_gate = upstream * pre_up * s * (1.0 + pre_gate * (1.0 - s))
        pair[:, at : at + tile] = grad_gate.astype(BF16)
        pair[:, hidden + at : hidden + at + tile] = grad_up.astype(BF16)
        pair_t[at : at + tile, :] = grad_gate.T.astype(BF16)
        pair_t[hidden + at : hidden + at + tile, :] = grad_up.T.astype(BF16)

    per_quarter = nx * CORES // QUARTERS
    for q in range(QUARTERS):
        parts = [dot(pair[...], full_w[q * per_quarter + i]) for i in range(per_quarter)]
        part = jnp.concatenate(parts, axis=1).astype(BF16)
        for g in range(groups):
            rows_r[g * GROUP + q] = part[g * span : (g + 1) * span]

    def order_back(g, _):
        part = rows_r[pl.ds(g * GROUP, GROUP)].reshape(GROUP * block, quarter)
        part = dot(swap[...], part).astype(BF16)
        rows_s[pl.ds(g * GROUP, GROUP)] = part.reshape(GROUP, block, quarter)
        return 0

    lax.fori_loop(0, groups, order_back, 0)
    spread(BACK, lambda e: rows_s.at[e], lambda s: back_r.at[s])

    chunk = min(384, 2 * hidden)

    def weight_grad(j):
        at = pl.multiple_of(j * cols, cols)

        def rows_of(r, _):
            spot = pl.ds(pl.multiple_of(r * chunk, chunk), chunk)
            grads[j, spot, :] = dot(pair_t[spot, :], x_mat[:, pl.ds(at, cols)]).astype(BF16)
            return 0

        lax.fori_loop(0, 2 * hidden // chunk, rows_of, 0)

    def halve(d):
        return pltpu.make_async_remote_copy(
            src_ref=grads.at[lax.rem(x + d, nx) * CORES + 1 - core],
            dst_ref=half_r.at[d - 1],
            send_sem=half_send.at[d - 1],
            recv_sem=half_recv.at[d - 1],
            device_id=(twin, me),
            device_id_type=MESH,
        )

    def pass_on(d):
        return pltpu.make_async_remote_copy(
            src_ref=grads.at[x_peer(d)],
            dst_ref=quarter_r.at[d - 1],
            send_sem=sum_send.at[d - 1],
            recv_sem=sum_recv.at[d - 1],
            device_id=(x_peer(d), me),
            device_id_type=MESH,
        )

    for d in range(1, nx + 1):
        weight_grad(lax.rem(x + d, nx) * CORES + 1 - core)
        halve(d).start()
    for d in range(1, nx + 1):
        weight_grad(x_peer(d))
        halve(d).wait_recv()
        if d < nx:

            def add(r, _):
                spot = pl.ds(pl.multiple_of(r * chunk, chunk), chunk)
                both = grads[x_peer(d), spot, :].astype(F32) + half_r[d - 1, spot, :].astype(F32)
                grads[x_peer(d), spot, :] = both.astype(BF16)
                return 0

            lax.fori_loop(0, 2 * hidden // chunk, add, 0)
            pass_on(d).start()

    for d in range(1, nx):
        pass_on(d).wait_recv()
    arrived(M1, m1_r)
    arrived(M2, m2_r)

    rows = GROUP * per_source

    def adam(i, _):
        for a in range(2):
            spot = pl.ds(a * hidden + i * rows, rows)
            total = grads[dp, spot, :].astype(F32) + half_r[nx - 1, spot, :].astype(F32)
            for d in range(nx - 1):
                total += quarter_r[d, spot, :].astype(F32)
            gradient = total * (1.0 / loss_scale)
            first = m1_r[a, pl.ds(i * GROUP, GROUP)].astype(F32).reshape(rows, cols)
            second = m2_r[a, pl.ds(i * GROUP, GROUP)].astype(F32).reshape(rows, cols)
            first = beta_one * first + (1.0 - beta_one) * gradient
            second = beta_two * second + (1.0 - beta_two) * gradient * gradient
            weight = full_w[dp, spot, :].astype(F32)
            weight = weight - step_size * first / (jnp.sqrt(second) + adam_eps)
            out = pl.ds(i * rows, rows)
            w_out[a, out, :] = weight.astype(BF16)
            m1_out[a, out, :] = first.astype(BF16)
            m2_out[a, out, :] = second.astype(BF16)
        return 0

    lax.fori_loop(0, groups, adam, 0)

    piece = lax.broadcasted_iota(jnp.int32, (tok, n * block), 1)

    arrived(BACK, back_r)
    returned = back_r[...].reshape(n * block, quarter)
    for q in range(QUARTERS):
        pick = (piece == spots[0] + q * cap) | (piece == spots[1] + q * cap)
        token_out[:, q * quarter : (q + 1) * quarter] = dot(pick.astype(BF16), returned).astype(BF16)

    for d in range(1, nx):
        gather(d).wait_send()
        pass_on(d).wait_send()
    for d in range(nx):
        hand_over(d).wait_send()
        halve(d + 1).wait_send()
    left(M1, m1_r.at[:, pl.ds(0, n - 1)])
    left(M2, m2_r.at[:, pl.ds(0, n - 1)])
    left(BACK, rows_s.at[pl.ds(0, n - 1)])


def place(*refs):
    count = (len(refs) - 1) // 2
    copies = [
        pltpu.make_async_copy(refs[i], refs[count + i], refs[-1].at[i]) for i in range(count)
    ]
    for copy in copies:
        copy.start()
    for copy in copies:
        copy.wait()


def per_device(
    mesh_sizes, tokens, routes, router_gates, hidden_cotangent, weights, first_moment, second_moment
):
    ndp, n = mesh_sizes
    nx = ndp // CORES
    nz = min(8, n)
    ny = n // nz
    tok, width = tokens.shape
    hidden = hidden_cotangent.shape[2]
    cap = 3 * tok * 2 // (2 * n)
    per_source, cols = weights.shape[2], weights.shape[3]
    block, cot_block, slots = QUARTERS * cap, HALVES * cap, n * cap
    vmem = pl.BlockSpec(memory_space=pltpu.VMEM)
    hbm = pl.BlockSpec(memory_space=pl.ANY)
    shapes = [(tok, width)] + [(2, hidden, cols)] * 3
    dma = pltpu.SemaphoreType.DMA
    results = pl.pallas_call(
        functools.partial(kernel, nx, ny, nz, cap),
        out_shape=tuple(pltpu.VMEM(shape, BF16) for shape in shapes),
        in_specs=[vmem] * 4 + [hbm] * 3,
        out_specs=(vmem,) * 4,
        scratch_shapes=[
            pltpu.VMEM((n, block, width // QUARTERS), BF16),
            pltpu.VMEM((n, block, width // QUARTERS), BF16),
            pltpu.VMEM((n, cot_block, hidden // HALVES), BF16),
            pltpu.VMEM((n, cot_block, hidden // HALVES), BF16),
            pltpu.VMEM((tok, 2 * hidden), BF16),
            pltpu.VMEM((2, n, per_source, cols), BF16),
            pltpu.VMEM((2, n, per_source, cols), BF16),
            pltpu.VMEM((2, n, per_source, cols), BF16),
            pltpu.VMEM((ndp, 2 * hidden, cols), BF16),
            pltpu.VMEM((slots, width), BF16),
            pltpu.VMEM((slots, hidden), BF16),
            pltpu.VMEM((slots, 2 * hidden), BF16),
            pltpu.VMEM((2 * hidden, slots), BF16),
            pltpu.VMEM((n, block, width // QUARTERS), BF16),
            pltpu.VMEM((ndp, 2 * hidden, cols), BF16),
            pltpu.VMEM((nx, 2 * hidden, cols), BF16),
            pltpu.VMEM((nx - 1, 2 * hidden, cols), BF16),
            pltpu.VMEM((GROUP * block,) * 2, BF16),
            pltpu.VMEM((GROUP * cot_block,) * 2, BF16),
            dma((6,)),
            dma((6,)),
            dma((nx - 1,)),
            dma((nx - 1,)),
            dma((nx,)),
            dma((nx,)),
            dma((nx,)),
            dma((nx,)),
            dma((nx - 1,)),
            dma((nx - 1,)),
        ],
        compiler_params=pltpu.CompilerParams(
            collective_id=0, has_side_effects=True, vmem_limit_bytes=50 * 1024 * 1024
        ),
        name="experts_step",
    )(
        routes.T,
        router_gates.T,
        tokens,
        hidden_cotangent,
        weights,
        first_moment,
        second_moment,
    )
    token_grads, new_w, new_first, new_second = pl.pallas_call(
        place,
        out_shape=tuple(jax.ShapeDtypeStruct(shape, BF16) for shape in shapes),
        in_specs=[vmem] * 4,
        out_specs=(hbm,) * 4,
        scratch_shapes=[dma((4,))],
        compiler_params=pltpu.CompilerParams(vmem_limit_bytes=1024 * 1024),
        name="place",
    )(*(pltpu.with_memory_space_constraint(result, pltpu.VMEM) for result in results))
    shape = (2, 1, hidden, cols)
    return token_grads, new_w.reshape(shape), new_first.reshape(shape), new_second.reshape(shape)


def solution(mesh):
    placed = (
        P(("dp", "expert"), None),
        P(("dp", "expert"), None),
        P(("dp", "expert"), None),
        P(("dp", "expert"), None, None),
        P(None, None, "expert", "dp"),
        P(None, None, "expert", "dp"),
        P(None, None, "expert", "dp"),
    )
    return jax.shard_map(
        functools.partial(per_device, (mesh.shape["dp"], mesh.shape["expert"])),
        mesh=mesh,
        in_specs=placed,
        out_specs=(
            P(("dp", "expert"), None),
            P(None, "expert", None, "dp"),
            P(None, "expert", None, "dp"),
            P(None, "expert", None, "dp"),
        ),
        check_vma=False,
    )
```

```python
import functools

import jax
import jax.numpy as jnp
from jax import lax
from jax.experimental import pallas as pl
from jax.experimental.pallas import tpu as pltpu
from jax.sharding import PartitionSpec as P

gate_unit = 32768.0
loss_scale = 16.0
beta_one = 0.9
beta_two = 0.95
step_size = 0.001
adam_eps = 1e-08

MESH = pl.DeviceIdType.MESH
F32 = jnp.float32
BF16 = jnp.bfloat16
CORES = 2
QUARTERS = 4
HALVES = 2
ALONG_Z = 8
GROUP = 4
W, ROWS, COTS, M1, M2, LONG, SHORT, OWN = range(8)


def dot(a, b, dims=((1,), (0,))):
    return lax.dot_general(a, b, (dims, ((), ())), preferred_element_type=F32)


def order_matrix(outer, inner, cap):
    size = outer * inner * cap
    row = lax.broadcasted_iota(jnp.int32, (size, size), 0)
    source = lax.broadcasted_iota(jnp.int32, (size, size), 1)
    a = sum((row >= i * inner * cap).astype(jnp.int32) for i in range(1, outer))
    rest = row - a * (inner * cap)
    b = sum((rest >= i * cap).astype(jnp.int32) for i in range(1, inner))
    return (source == b * (outer * cap) + a * cap + rest - b * cap).astype(BF16)


def kernel(
    nx,
    ny,
    nz,
    cap,
    routes,
    gates,
    tokens,
    cotangent,
    w,
    m1,
    m2,
    token_out,
    w_out,
    m1_out,
    m2_out,
    rows_s,
    rows_r,
    cots_s,
    cots_r,
    scaled,
    w_r,
    m1_r,
    m2_r,
    full_w,
    x_mat,
    cot_mat,
    pair,
    pair_t,
    back_r,
    grads,
    half_r,
    quarter_r,
    swap,
    fold,
    near_tokens,
    near_routes,
    near_back,
    picks_own,
    picks_far,
    picks_short,
    near_send,
    near_recv,
    bring_send,
    bring_recv,
    send,
    recv,
    gather_send,
    gather_recv,
    twin_send,
    twin_recv,
    half_send,
    half_recv,
    sum_send,
    sum_recv,
):
    n = ny * nz
    dp, me = lax.axis_index("dp"), lax.axis_index("expert")
    x, core = dp // CORES, dp % CORES
    y, z = me // nz, me % nz
    twin = x * CORES + 1 - core
    tok, width = tokens.shape
    hidden = cotangent.shape[2]
    quarter, half = width // QUARTERS, hidden // HALVES
    per_source, cols = w.shape[2], w.shape[3]
    block = QUARTERS * cap
    cot_block = HALVES * cap
    groups = n // GROUP
    span = GROUP * cap
    slots = n * cap

    def peer(i):
        step = i // ny
        dz = jnp.where(step % 2 == 1, (step + 1) // 2, nz - step // 2)
        return lax.rem(y + i % ny, ny) * nz + lax.rem(z + dz, nz)

    def x_peer(d):
        return lax.rem(x + d, nx) * CORES + core

    barrier = pltpu.get_barrier_semaphore()

    def greet(i, _):
        pl.semaphore_signal(barrier, inc=1, device_id=(dp, peer(i)), device_id_type=MESH)
        return 0

    lax.fori_loop(1, n, greet, 0)
    for d in range(1, nx):
        pl.semaphore_signal(barrier, inc=1, device_id=(x_peer(d), me), device_id_type=MESH)
    pl.semaphore_signal(barrier, inc=1, device_id=(twin, me), device_id_type=MESH)
    pl.semaphore_wait(barrier, n - 1 + nx - 1 + 1)

    def spread(kind, source, landing, parts=((ny, n), (1, ny))):
        def start(i, _):
            to = peer(i)
            pltpu.make_async_remote_copy(
                src_ref=source(to),
                dst_ref=landing(me),
                send_sem=send.at[kind],
                recv_sem=recv.at[kind],
                device_id=(dp, to),
                device_id_type=MESH,
            ).start()
            return 0

        for first, last in parts:
            lax.fori_loop(first, last, start, 0)
        pltpu.make_async_copy(source(me), landing(me), recv.at[kind]).start()

    def arrived(kind, ref):
        pltpu.make_async_copy(ref, ref, recv.at[kind]).wait()

    def left(kind, ref):
        pltpu.make_async_copy(ref, ref, send.at[kind]).wait()

    spread(W, lambda e: w.at[:, e], lambda s: w_r.at[:, s])

    side = 1 - 2 * core
    far = nz // 2
    short = nz - 1 - far

    def plane(step):
        return lax.rem(z + step + 2 * nz, nz)

    def lend(i):
        to = (dp, y * nz + plane(side * (1 - 2 * i)))
        return [
            pltpu.make_async_remote_copy(
                src_ref=source,
                dst_ref=landing.at[i],
                send_sem=near_send.at[2 * j + i],
                recv_sem=near_recv.at[2 * j + i],
                device_id=to,
                device_id_type=MESH,
            )
            for j, (source, landing) in enumerate(((tokens, near_tokens), (routes, near_routes)))
        ]

    for i in range(2):
        for copy in lend(i):
            copy.start()
    picks_of = (picks_far, picks_short)

    experts = n
    earlier = lax.broadcasted_iota(jnp.int32, (tok, tok), 0)
    later = lax.broadcasted_iota(jnp.int32, (tok, tok), 1)
    ids = lax.broadcasted_iota(jnp.int32, (experts, tok), 0)

    def number(ref):
        rows = [ref[k : k + 1, :] for k in range(2)]
        hot = [(ids == r).astype(F32) for r in rows]
        before = dot((hot[0] + hot[1]).astype(BF16), (earlier < later).astype(BF16))
        return rows, [jnp.sum(h * before, axis=0, keepdims=True).astype(jnp.int32) for h in hot]

    route_rows, pos_row = number(routes)

    def column(row):
        return jnp.sum(jnp.where(earlier == later, row, jnp.zeros_like(row)), axis=1, keepdims=True)

    for k in range(2):
        factor = column(gates[k : k + 1, :].astype(F32)) * (1.0 / gate_unit)
        scaled[:, k * hidden : (k + 1) * hidden] = (factor * cotangent[:, k, :].astype(F32)).astype(BF16)

    swap[...] = order_matrix(QUARTERS, GROUP, cap)
    fold[...] = order_matrix(HALVES, GROUP, cap)

    piece = lax.broadcasted_iota(jnp.int32, (ny * block, tok), 0)
    cot_piece = lax.broadcasted_iota(jnp.int32, (GROUP * cot_block, tok), 0)

    def pack_cots(g, _):
        first = g * (GROUP * cot_block)
        total = jnp.zeros((GROUP * cot_block, half), F32)
        for k in range(2):
            for h in range(HALVES):
                spot = route_rows[k] * cot_block + pos_row[k] + h * cap - first
                pick = (cot_piece == spot).astype(BF16)
                start = k * hidden + h * half
                total += dot(pick, scaled[:, start : start + half])
        cots_s[pl.ds(g * GROUP, GROUP)] = total.reshape(GROUP, cot_block, half).astype(BF16)
        return 0

    def pack_rows(first, count, sign, numbers, rows, picks):
        places = []
        for k, (r, p) in enumerate(zip(*numbers)):
            at_y = sum((r >= i * nz).astype(jnp.int32) for i in range(1, ny))
            places.append((r - at_y * nz, at_y * block + p))
        spots = []
        for at_z, at in places:
            step = sign * (at_z - z)
            step = jnp.where(step < 0, step + nz, step)
            spots.append(column(jnp.where(step < count, step * (ny * block) + at, -nz * ny * block)))
        position = lax.broadcasted_iota(jnp.int32, (tok, count * ny * block), 1)
        for q in range(QUARTERS):
            pick = (position == spots[0] + q * cap) | (position == spots[1] + q * cap)
            picks[q] = pick.astype(BF16)

        def pack(g, _):
            goal = plane(sign * g)
            total = jnp.zeros((ny * block, quarter), F32)
            for q in range(QUARTERS):
                spot = [jnp.where(at_z == goal, at + q * cap, -1) for at_z, at in places]
                pick = (piece == spot[0]) | (piece == spot[1])
                total += dot(pick.astype(BF16), rows[:, q * quarter : (q + 1) * quarter])
            rows_s[pl.ds((first + g) * ny, ny)] = total.astype(BF16).reshape(ny, block, quarter)
            return 0

        lax.fori_loop(0, count, pack, 0)

    def send_rows(first, count, sign, source_z):
        source = y * nz + source_z

        def start(g, i):
            at_y = lax.rem(y + i, ny)
            pltpu.make_async_remote_copy(
                src_ref=rows_s.at[(first + g) * ny + at_y],
                dst_ref=rows_r.at[source],
                send_sem=send.at[ROWS],
                recv_sem=recv.at[ROWS],
                device_id=(dp, at_y * nz + plane(sign * g)),
                device_id_type=MESH,
            ).start()
            return 0

        lax.fori_loop(ny, count * ny, lambda i, _: start(i // ny, i % ny), 0)
        lax.fori_loop(1, ny, lambda i, _: start(0, i), 0)
        pltpu.make_async_copy(rows_s.at[first * ny + y], rows_r.at[source], recv.at[ROWS]).start()

    lax.fori_loop(0, groups, pack_cots, 0)
    spread(COTS, lambda e: cots_s.at[e], lambda s: cots_r.at[s])
    pack_rows(0, 1, 1, (route_rows, pos_row), tokens, picks_own)
    send_rows(0, 1, 0, z)
    arrived(W, w_r)

    def own_columns(i, _):
        for a in range(2):
            part = w_r[a, pl.ds(i * GROUP, GROUP)].astype(F32)
            rows = GROUP * per_source
            full_w[dp, pl.ds(a * hidden + i * rows, rows), :] = part.reshape(rows, cols).astype(BF16)
        return 0

    lax.fori_loop(0, groups, own_columns, 0)

    def gather(d):
        return pltpu.make_async_remote_copy(
            src_ref=full_w.at[dp],
            dst_ref=full_w.at[dp],
            send_sem=gather_send.at[d - 1],
            recv_sem=gather_recv.at[d - 1],
            device_id=(x_peer(d), me),
            device_id_type=MESH,
        )

    def hand_over(d):
        held = lax.rem(x - d + nx, nx) * CORES + core
        return pltpu.make_async_remote_copy(
            src_ref=full_w.at[held],
            dst_ref=full_w.at[held],
            send_sem=twin_send.at[d],
            recv_sem=twin_recv.at[d],
            device_id=(twin, me),
            device_id_type=MESH,
        )

    for d in range(1, nx):
        gather(d).start()
    hand_over(0).start()

    for i, (first, count, sign) in enumerate(((1, far, side), (1 + far, short, -side))):
        for copy in lend(i):
            copy.wait_recv()
        pack_rows(first, count, sign, number(near_routes.at[i]), near_tokens.at[i], picks_of[i])
        send_rows(first, count, sign, plane(-sign))
    spread(M1, lambda e: m1.at[:, e], lambda s: m1_r.at[:, s])

    for d in range(1, nx):
        gather(d).wait_recv()
        hand_over(d).start()

    arrived(COTS, cots_r)

    def order_cots(g, _):
        part = cots_r[pl.ds(g * GROUP, GROUP)].astype(F32).reshape(GROUP * cot_block, half)
        part = dot(fold[...], part.astype(BF16)).astype(BF16)
        for h in range(HALVES):
            cot_mat[pl.ds(g * span, span), h * half : (h + 1) * half] = part[h * span : (h + 1) * span]
        return 0

    lax.fori_loop(0, groups, order_cots, 0)
    arrived(ROWS, rows_r)

    def order_rows(g, _):
        part = rows_r[pl.ds(g * GROUP, GROUP)].reshape(GROUP * block, quarter)
        part = dot(swap[...], part).astype(BF16)
        for q in range(QUARTERS):
            x_mat[pl.ds(g * span, span), q * quarter : (q + 1) * quarter] = part[q * span : (q + 1) * span]
        return 0

    lax.fori_loop(0, groups, order_rows, 0)

    for d in range(nx):
        hand_over(d).wait_recv()

    tile = min(256, hidden)
    for t in range(hidden // tile):
        at = t * tile
        gate_w = jnp.concatenate([full_w[j, at : at + tile] for j in range(nx * CORES)], axis=1)
        pre_gate = dot(x_mat[...], gate_w, ((1,), (1,)))
        at += hidden
        up_w = jnp.concatenate([full_w[j, at : at + tile] for j in range(nx * CORES)], axis=1)
        pre_up = dot(x_mat[...], up_w, ((1,), (1,)))
        at -= hidden
        s = jax.nn.sigmoid(pre_gate)
        upstream = cot_mat[:, at : at + tile].astype(F32)
        grad_up = upstream * pre_gate * s
        grad_gate = upstream * pre_up * s * (1.0 + pre_gate * (1.0 - s))
        pair[:, at : at + tile] = grad_gate.astype(BF16)
        pair[:, hidden + at : hidden + at + tile] = grad_up.astype(BF16)
        pair_t[at : at + tile, :] = grad_gate.T.astype(BF16)
        pair_t[hidden + at : hidden + at + tile, :] = grad_up.T.astype(BF16)

    per_quarter = nx * CORES // QUARTERS
    for q in range(QUARTERS):
        parts = [dot(pair[...], full_w[q * per_quarter + i]) for i in range(per_quarter)]
        part = jnp.concatenate(parts, axis=1).astype(BF16)
        for g in range(groups):
            rows_r[g * GROUP + q] = part[g * span : (g + 1) * span]

    left(W, w_r.at[:, pl.ds(0, n - 1)])
    left(COTS, cots_s.at[pl.ds(0, n - 1)])
    left(ROWS, rows_s.at[pl.ds(0, n - 3)])

    def order_back(g, _):
        part = rows_r[pl.ds(g * GROUP, GROUP)].reshape(GROUP * block, quarter)
        part = dot(swap[...], part).astype(BF16)
        rows_s[pl.ds(g * GROUP, GROUP)] = part.reshape(GROUP, block, quarter)
        return 0

    lax.fori_loop(0, groups, order_back, 0)

    def send_back(kind, first, count, sign):
        def start(g, i):
            at_y = lax.rem(y + i, ny)
            pltpu.make_async_remote_copy(
                src_ref=rows_s.at[at_y * nz + plane(-sign * (g + min(first, 1)))],
                dst_ref=back_r.at[(first + g) * ny + y],
                send_sem=send.at[kind],
                recv_sem=recv.at[kind],
                device_id=(dp, at_y * nz + plane(-sign * g)),
                device_id_type=MESH,
            ).start()
            return 0

        lax.fori_loop(ny, count * ny, lambda i, _: start(i // ny, i % ny), 0)
        lax.fori_loop(1, ny, lambda i, _: start(0, i), 0)
        pltpu.make_async_copy(
            rows_s.at[y * nz + plane(-sign * min(first, 1))],
            back_r.at[first * ny + y],
            recv.at[kind],
        ).start()

    sides = ((1, far, side), (1 + far, short, -side))
    send_back(LONG, *sides[0])
    send_back(SHORT, *sides[1])
    send_back(OWN, 0, 1, 0)
    spread(M2, lambda e: m2.at[:, e], lambda s: m2_r.at[:, s])

    chunk = min(384, 2 * hidden)

    def weight_grad(k):
        at = pl.multiple_of(k * CORES * cols, CORES * cols)

        def rows_of(r, _):
            spot = pl.ds(pl.multiple_of(r * chunk, chunk), chunk)
            part = dot(pair_t[spot, :], x_mat[:, pl.ds(at, CORES * cols)]).astype(BF16)
            for i in range(CORES):
                grads[k * CORES + i, spot, :] = part[:, i * cols : (i + 1) * cols]
            return 0

        lax.fori_loop(0, 2 * hidden // chunk, rows_of, 0)

    def halve(d):
        return pltpu.make_async_remote_copy(
            src_ref=grads.at[lax.rem(x + d, nx) * CORES + 1 - core],
            dst_ref=half_r.at[d - 1],
            send_sem=half_send.at[d - 1],
            recv_sem=half_recv.at[d - 1],
            device_id=(twin, me),
            device_id_type=MESH,
        )

    def pass_on(d):
        return pltpu.make_async_remote_copy(
            src_ref=grads.at[x_peer(d)],
            dst_ref=quarter_r.at[d - 1],
            send_sem=sum_send.at[d - 1],
            recv_sem=sum_recv.at[d - 1],
            device_id=(x_peer(d), me),
            device_id_type=MESH,
        )

    for d in range(1, nx + 1):
        weight_grad(lax.rem(x + d, nx))
        halve(d).start()
    for d in range(1, nx + 1):
        halve(d).wait_recv()
        if d < nx:

            def add(r, _):
                spot = pl.ds(pl.multiple_of(r * chunk, chunk), chunk)
                both = grads[x_peer(d), spot, :].astype(F32) + half_r[d - 1, spot, :].astype(F32)
                grads[x_peer(d), spot, :] = both.astype(BF16)
                return 0

            lax.fori_loop(0, 2 * hidden // chunk, add, 0)
            pass_on(d).start()

    def sums(first, count, picks, out):
        for q in range(QUARTERS):
            part = back_r[first * ny : (first + count) * ny].reshape(count * ny * block, quarter)
            out(slice(q * quarter, (q + 1) * quarter), dot(picks[q], part))

    def bring(i):
        return pltpu.make_async_remote_copy(
            src_ref=near_tokens.at[i],
            dst_ref=near_back.at[i],
            send_sem=bring_send.at[i],
            recv_sem=bring_recv.at[i],
            device_id=(dp, y * nz + plane(-sides[i][2])),
            device_id_type=MESH,
        )

    for i, kind in enumerate((LONG, SHORT)):
        first, count, sign = sides[i]

        def keep(spot, total, i=i):
            near_tokens[i, :, spot] = total.astype(BF16)

        arrived(kind, back_r.at[pl.ds(first * ny, count * ny)])
        sums(first, count, picks_of[i], keep)
        bring(i).start()

    for d in range(1, nx):
        pass_on(d).wait_recv()
    arrived(M1, m1_r)
    arrived(M2, m2_r)

    rows = GROUP * per_source

    def adam(i, _):
        for a in range(2):
            spot = pl.ds(a * hidden + i * rows, rows)
            total = grads[dp, spot, :].astype(F32) + half_r[nx - 1, spot, :].astype(F32)
            for d in range(nx - 1):
                total += quarter_r[d, spot, :].astype(F32)
            gradient = total * (1.0 / loss_scale)
            first = m1_r[a, pl.ds(i * GROUP, GROUP)].astype(F32).reshape(rows, cols)
            second = m2_r[a, pl.ds(i * GROUP, GROUP)].astype(F32).reshape(rows, cols)
            first = beta_one * first + (1.0 - beta_one) * gradient
            second = beta_two * second + (1.0 - beta_two) * gradient * gradient
            weight = full_w[dp, spot, :].astype(F32)
            weight = weight - step_size * first / (jnp.sqrt(second) + adam_eps)
            out = pl.ds(i * rows, rows)
            w_out[a, out, :] = weight.astype(BF16)
            m1_out[a, out, :] = first.astype(BF16)
            m2_out[a, out, :] = second.astype(BF16)
        return 0

    lax.fori_loop(0, groups, adam, 0)

    arrived(OWN, back_r.at[pl.ds(0, ny)])
    for i in range(2):
        bring(i).wait_recv()

    def finish(spot, total):
        for i in range(2):
            total += near_back[i, :, spot].astype(F32)
        token_out[:, spot] = total.astype(BF16)

    sums(0, 1, picks_own, finish)

    for i in range(2):
        for copy in lend(i):
            copy.wait_send()
    for d in range(1, nx):
        gather(d).wait_send()
        pass_on(d).wait_send()
    for d in range(nx):
        hand_over(d).wait_send()
        halve(d + 1).wait_send()
    left(M1, m1_r.at[:, pl.ds(0, n - 1)])
    left(M2, m2_r.at[:, pl.ds(0, n - 1)])
    left(LONG, rows_s.at[pl.ds(0, far * ny - 1)])
    left(SHORT, rows_s.at[pl.ds(0, short * ny - 1)])
    left(OWN, rows_s.at[pl.ds(0, ny - 1)])
    for i in range(2):
        bring(i).wait_send()


def place(*refs):
    count = (len(refs) - 1) // 2
    copies = [
        pltpu.make_async_copy(refs[i], refs[count + i], refs[-1].at[i]) for i in range(count)
    ]
    for copy in copies:
        copy.start()
    for copy in copies:
        copy.wait()


def per_device(
    mesh_sizes, tokens, routes, router_gates, hidden_cotangent, weights, first_moment, second_moment
):
    ndp, n = mesh_sizes
    nx = ndp // CORES
    nz = ALONG_Z
    ny = n // nz
    tok, width = tokens.shape
    hidden = hidden_cotangent.shape[2]
    cap = 3 * tok * 2 // (2 * n)
    per_source, cols = weights.shape[2], weights.shape[3]
    block, cot_block, slots = QUARTERS * cap, HALVES * cap, n * cap
    plane = ny * block
    vmem = pl.BlockSpec(memory_space=pltpu.VMEM)
    hbm = pl.BlockSpec(memory_space=pl.ANY)
    shapes = [(tok, width)] + [(2, hidden, cols)] * 3
    dma = pltpu.SemaphoreType.DMA
    results = pl.pallas_call(
        functools.partial(kernel, nx, ny, nz, cap),
        out_shape=tuple(pltpu.VMEM(shape, BF16) for shape in shapes),
        in_specs=[vmem] * 4 + [hbm] * 3,
        out_specs=(vmem,) * 4,
        scratch_shapes=[
            pltpu.VMEM((n, block, width // QUARTERS), BF16),
            pltpu.VMEM((n, block, width // QUARTERS), BF16),
            pltpu.VMEM((n, cot_block, hidden // HALVES), BF16),
            pltpu.VMEM((n, cot_block, hidden // HALVES), BF16),
            pltpu.VMEM((tok, 2 * hidden), BF16),
            pltpu.VMEM((2, n, per_source, cols), BF16),
            pltpu.VMEM((2, n, per_source, cols), BF16),
            pltpu.VMEM((2, n, per_source, cols), BF16),
            pltpu.VMEM((ndp, 2 * hidden, cols), BF16),
            pltpu.VMEM((slots, width), BF16),
            pltpu.VMEM((slots, hidden), BF16),
            pltpu.VMEM((slots, 2 * hidden), BF16),
            pltpu.VMEM((2 * hidden, slots), BF16),
            pltpu.VMEM((n, block, width // QUARTERS), BF16),
            pltpu.VMEM((ndp, 2 * hidden, cols), BF16),
            pltpu.VMEM((nx, 2 * hidden, cols), BF16),
            pltpu.VMEM((nx - 1, 2 * hidden, cols), BF16),
            pltpu.VMEM((GROUP * block,) * 2, BF16),
            pltpu.VMEM((GROUP * cot_block,) * 2, BF16),
            pltpu.VMEM((2, tok, width), BF16),
            pltpu.VMEM((2, 2, tok), jnp.int32),
            pltpu.VMEM((2, tok, width), BF16),
            pltpu.VMEM((QUARTERS, tok, plane), BF16),
            pltpu.VMEM((QUARTERS, tok, nz // 2 * plane), BF16),
            pltpu.VMEM((QUARTERS, tok, (nz - 1 - nz // 2) * plane), BF16),
            dma((4,)),
            dma((4,)),
            dma((2,)),
            dma((2,)),
            dma((8,)),
            dma((8,)),
            dma((nx - 1,)),
            dma((nx - 1,)),
            dma((nx,)),
            dma((nx,)),
            dma((nx,)),
            dma((nx,)),
            dma((nx - 1,)),
            dma((nx - 1,)),
        ],
        compiler_params=pltpu.CompilerParams(
            collective_id=0, has_side_effects=True, vmem_limit_bytes=53 * 1024 * 1024
        ),
        name="experts_step",
    )(
        routes.T,
        router_gates.T,
        tokens,
        hidden_cotangent,
        weights,
        first_moment,
        second_moment,
    )
    token_grads, new_w, new_first, new_second = pl.pallas_call(
        place,
        out_shape=tuple(jax.ShapeDtypeStruct(shape, BF16) for shape in shapes),
        in_specs=[vmem] * 4,
        out_specs=(hbm,) * 4,
        scratch_shapes=[dma((4,))],
        compiler_params=pltpu.CompilerParams(vmem_limit_bytes=1024 * 1024),
        name="place",
    )(*(pltpu.with_memory_space_constraint(result, pltpu.VMEM) for result in results))
    shape = (2, 1, hidden, cols)
    return token_grads, new_w.reshape(shape), new_first.reshape(shape), new_second.reshape(shape)


def solution(mesh):
    placed = (
        P(("dp", "expert"), None),
        P(("dp", "expert"), None),
        P(("dp", "expert"), None),
        P(("dp", "expert"), None, None),
        P(None, None, "expert", "dp"),
        P(None, None, "expert", "dp"),
        P(None, None, "expert", "dp"),
    )
    return jax.shard_map(
        functools.partial(per_device, (mesh.shape["dp"], mesh.shape["expert"])),
        mesh=mesh,
        in_specs=placed,
        out_specs=(
            P(("dp", "expert"), None),
            P(None, "expert", None, "dp"),
            P(None, "expert", None, "dp"),
            P(None, "expert", None, "dp"),
        ),
        check_vma=False,
    )
```

```python
import functools

import jax
import jax.numpy as jnp
from jax import lax
from jax.experimental import pallas as pl
from jax.experimental.pallas import tpu as pltpu
from jax.sharding import PartitionSpec as P

gate_unit = 32768.0
loss_scale = 16.0
beta_one = 0.9
beta_two = 0.95
step_size = 0.001
adam_eps = 1e-08

MESH = pl.DeviceIdType.MESH
F32 = jnp.float32
BF16 = jnp.bfloat16
CORES = 2
PIECES = 4
QUARTERS = 4
HALVES = 2
ALONG_Z = 8
GROUP = 4
W, ROWS, COTS, LONG, SHORT, OWN, STATE = range(7)
STATES = ((0, 0), (0, 1), (1, 0), (1, 1))
EARLY, MIDDLE, LATE = (), (0, 1, 2), (3,)


def dot(a, b, dims=((1,), (0,))):
    return lax.dot_general(a, b, (dims, ((), ())), preferred_element_type=F32)


def order_matrix(outer, inner, cap):
    size = outer * inner * cap
    row = lax.broadcasted_iota(jnp.int32, (size, size), 0)
    source = lax.broadcasted_iota(jnp.int32, (size, size), 1)
    a = sum((row >= i * inner * cap).astype(jnp.int32) for i in range(1, outer))
    rest = row - a * (inner * cap)
    b = sum((rest >= i * cap).astype(jnp.int32) for i in range(1, inner))
    return (source == b * (outer * cap) + a * cap + rest - b * cap).astype(BF16)


def kernel(
    nx,
    ny,
    nz,
    cap,
    routes,
    gates,
    tokens_hbm,
    cotangent_hbm,
    w,
    m1,
    m2,
    token_out,
    w_out,
    m1_out,
    m2_out,
    rows_s,
    rows_r,
    cots_s,
    cots_r,
    tokens,
    cotangent,
    scaled,
    w_r,
    m1_r,
    m2_r,
    full_w,
    x_mat,
    cot_mat,
    pair,
    pair_t,
    back_r,
    grads,
    half_r,
    quarter_r,
    swap,
    fold,
    near_tokens,
    near_routes,
    near_back,
    picks_own,
    picks_far,
    picks_short,
    own_sum,
    load_sem,
    near_send,
    near_recv,
    bring_send,
    bring_recv,
    send,
    recv,
    gather_send,
    gather_recv,
    twin_send,
    twin_recv,
    half_send,
    half_recv,
    sum_send,
    sum_recv,
):
    n = ny * nz
    dp, me = lax.axis_index("dp"), lax.axis_index("expert")
    x, core = dp // CORES, dp % CORES
    y, z = me // nz, me % nz
    twin = x * CORES + 1 - core
    tok, width = tokens.shape
    hidden = cotangent.shape[2]
    quarter, half = width // QUARTERS, hidden // HALVES
    per_source, cols = w.shape[2], w.shape[3]
    block = QUARTERS * cap
    cot_block = HALVES * cap
    groups = n // GROUP
    span = GROUP * cap
    slots = n * cap

    def peer(i):
        step = i // ny
        dz = jnp.where(step % 2 == 1, (step + 1) // 2, nz - step // 2)
        return lax.rem(y + i % ny, ny) * nz + lax.rem(z + dz, nz)

    def x_peer(d):
        return lax.rem(x + d, nx) * CORES + core

    loads = [
        pltpu.make_async_copy(source, landing, load_sem.at[i])
        for i, (source, landing) in enumerate(((tokens_hbm, tokens), (cotangent_hbm, cotangent)))
    ]
    for load in loads:
        load.start()

    barrier = pltpu.get_barrier_semaphore()

    def greet(i, _):
        pl.semaphore_signal(barrier, inc=1, device_id=(dp, peer(i)), device_id_type=MESH)
        return 0

    lax.fori_loop(1, n, greet, 0)
    for d in range(1, nx):
        pl.semaphore_signal(barrier, inc=1, device_id=(x_peer(d), me), device_id_type=MESH)
    pl.semaphore_signal(barrier, inc=1, device_id=(twin, me), device_id_type=MESH)
    pl.semaphore_wait(barrier, n - 1 + nx - 1 + 1)

    def spread(kind, source, landing, parts=((ny, n), (1, ny))):
        def start(i, _):
            to = peer(i)
            pltpu.make_async_remote_copy(
                src_ref=source(to),
                dst_ref=landing(me),
                send_sem=send.at[kind],
                recv_sem=recv.at[kind],
                device_id=(dp, to),
                device_id_type=MESH,
            ).start()
            return 0

        for first, last in parts:
            lax.fori_loop(first, last, start, 0)
        pltpu.make_async_copy(source(me), landing(me), recv.at[kind]).start()

    def arrived(kind, ref):
        pltpu.make_async_copy(ref, ref, recv.at[kind]).wait()

    def left(kind, ref):
        pltpu.make_async_copy(ref, ref, send.at[kind]).wait()

    spread(W, lambda e: w.at[:, e], lambda s: w_r.at[:, s])

    side = 1 - 2 * core
    far = nz // 2
    short = nz - 1 - far

    def plane(step):
        return lax.rem(z + step + 2 * nz, nz)

    def lend(source, landing, kind, i):
        return pltpu.make_async_remote_copy(
            src_ref=source,
            dst_ref=landing,
            send_sem=near_send.at[2 * kind + i],
            recv_sem=near_recv.at[2 * kind + i],
            device_id=(dp, y * nz + plane(side * (1 - 2 * i))),
            device_id_type=MESH,
        )

    def lent(i):
        return [
            lend(tokens_hbm, near_tokens.at[i], 0, i),
            lend(routes, near_routes.at[i], 1, i),
        ]

    piece_rows = tok // PIECES
    for i in range(2):
        for j in range(PIECES):
            rows = pl.ds(j * piece_rows, piece_rows)
            lend(tokens_hbm.at[rows], near_tokens.at[i, rows], 0, i).start()
        lend(routes, near_routes.at[i], 1, i).start()
    picks_of = (picks_far, picks_short)

    experts = n
    earlier = lax.broadcasted_iota(jnp.int32, (tok, tok), 0)
    later = lax.broadcasted_iota(jnp.int32, (tok, tok), 1)
    ids = lax.broadcasted_iota(jnp.int32, (experts, tok), 0)

    def number(ref):
        rows = [ref[k : k + 1, :] for k in range(2)]
        hot = [(ids == r).astype(F32) for r in rows]
        before = dot((hot[0] + hot[1]).astype(BF16), (earlier < later).astype(BF16))
        return rows, [jnp.sum(h * before, axis=0, keepdims=True).astype(jnp.int32) for h in hot]

    route_rows, pos_row = number(routes)
    for load in loads:
        load.wait()

    def column(row):
        return jnp.sum(jnp.where(earlier == later, row, jnp.zeros_like(row)), axis=1, keepdims=True)

    for k in range(2):
        factor = column(gates[k : k + 1, :].astype(F32)) * (1.0 / gate_unit)
        scaled[:, k * hidden : (k + 1) * hidden] = (factor * cotangent[:, k, :].astype(F32)).astype(BF16)

    swap[...] = order_matrix(QUARTERS, GROUP, cap)
    fold[...] = order_matrix(HALVES, GROUP, cap)

    piece = lax.broadcasted_iota(jnp.int32, (ny * block, tok), 0)
    cot_piece = lax.broadcasted_iota(jnp.int32, (GROUP * cot_block, tok), 0)

    def pack_cots(g, _):
        first = g * (GROUP * cot_block)
        total = jnp.zeros((GROUP * cot_block, half), F32)
        for k in range(2):
            for h in range(HALVES):
                spot = route_rows[k] * cot_block + pos_row[k] + h * cap - first
                pick = (cot_piece == spot).astype(BF16)
                start = k * hidden + h * half
                total += dot(pick, scaled[:, start : start + half])
        cots_s[pl.ds(g * GROUP, GROUP)] = total.reshape(GROUP, cot_block, half).astype(BF16)
        return 0

    def pack_rows(first, count, sign, numbers, rows, picks):
        places = []
        for k, (r, p) in enumerate(zip(*numbers)):
            at_y = sum((r >= i * nz).astype(jnp.int32) for i in range(1, ny))
            places.append((r - at_y * nz, at_y * block + p))
        spots = []
        for at_z, at in places:
            step = sign * (at_z - z)
            step = jnp.where(step < 0, step + nz, step)
            spots.append(column(jnp.where(step < count, step * (ny * block) + at, -nz * ny * block)))
        position = lax.broadcasted_iota(jnp.int32, (tok, count * ny * block), 1)
        for q in range(QUARTERS):
            pick = (position == spots[0] + q * cap) | (position == spots[1] + q * cap)
            picks[q] = pick.astype(BF16)

        def pack(g, _):
            goal = plane(sign * g)
            total = jnp.zeros((ny * block, quarter), F32)
            for q in range(QUARTERS):
                spot = [jnp.where(at_z == goal, at + q * cap, -1) for at_z, at in places]
                pick = (piece == spot[0]) | (piece == spot[1])
                total += dot(pick.astype(BF16), rows[:, q * quarter : (q + 1) * quarter])
            rows_s[pl.ds((first + g) * ny, ny)] = total.astype(BF16).reshape(ny, block, quarter)
            return 0

        lax.fori_loop(0, count, pack, 0)

    def send_rows(first, count, sign, source_z):
        source = y * nz + source_z

        def start(g, i):
            at_y = lax.rem(y + i, ny)
            pltpu.make_async_remote_copy(
                src_ref=rows_s.at[(first + g) * ny + at_y],
                dst_ref=rows_r.at[source],
                send_sem=send.at[ROWS],
                recv_sem=recv.at[ROWS],
                device_id=(dp, at_y * nz + plane(sign * g)),
                device_id_type=MESH,
            ).start()
            return 0

        lax.fori_loop(ny, count * ny, lambda i, _: start(i // ny, i % ny), 0)
        lax.fori_loop(1, ny, lambda i, _: start(0, i), 0)
        pltpu.make_async_copy(rows_s.at[first * ny + y], rows_r.at[source], recv.at[ROWS]).start()

    lax.fori_loop(0, groups, pack_cots, 0)
    spread(COTS, lambda e: cots_s.at[e], lambda s: cots_r.at[s])
    moments = ((m1, m1_r), (m2, m2_r))

    def spread_states(which):
        for i in which:
            moment, a = STATES[i]
            source, landing = moments[moment]
            spread(
                STATE + i,
                lambda e, source=source, a=a: source.at[a, e],
                lambda s, landing=landing, a=a: landing.at[a, s],
            )

    spread_states(EARLY)
    pack_rows(0, 1, 1, (route_rows, pos_row), tokens, picks_own)
    send_rows(0, 1, 0, z)
    arrived(W, w_r)

    def own_columns(i, _):
        for a in range(2):
            part = w_r[a, pl.ds(i * GROUP, GROUP)].astype(F32)
            rows = GROUP * per_source
            full_w[dp, pl.ds(a * hidden + i * rows, rows), :] = part.reshape(rows, cols).astype(BF16)
        return 0

    lax.fori_loop(0, groups, own_columns, 0)

    def gather(d):
        return pltpu.make_async_remote_copy(
            src_ref=full_w.at[dp],
            dst_ref=full_w.at[dp],
            send_sem=gather_send.at[d - 1],
            recv_sem=gather_recv.at[d - 1],
            device_id=(x_peer(d), me),
            device_id_type=MESH,
        )

    def hand_over(d):
        held = lax.rem(x - d + nx, nx) * CORES + core
        return pltpu.make_async_remote_copy(
            src_ref=full_w.at[held],
            dst_ref=full_w.at[held],
            send_sem=twin_send.at[d],
            recv_sem=twin_recv.at[d],
            device_id=(twin, me),
            device_id_type=MESH,
        )

    for d in range(1, nx):
        gather(d).start()
    hand_over(0).start()

    for i, (first, count, sign) in enumerate(((1, far, side), (1 + far, short, -side))):
        for copy in lent(i):
            copy.wait_recv()
        pack_rows(first, count, sign, number(near_routes.at[i]), near_tokens.at[i], picks_of[i])
        send_rows(first, count, sign, plane(-sign))
    spread_states(MIDDLE)

    for d in range(1, nx):
        gather(d).wait_recv()
        hand_over(d).start()

    arrived(COTS, cots_r)

    def order_cots(g, _):
        part = cots_r[pl.ds(g * GROUP, GROUP)].astype(F32).reshape(GROUP * cot_block, half)
        part = dot(fold[...], part.astype(BF16)).astype(BF16)
        for h in range(HALVES):
            cot_mat[pl.ds(g * span, span), h * half : (h + 1) * half] = part[h * span : (h + 1) * span]
        return 0

    lax.fori_loop(0, groups, order_cots, 0)
    arrived(ROWS, rows_r)

    def order_rows(g, _):
        part = rows_r[pl.ds(g * GROUP, GROUP)].reshape(GROUP * block, quarter)
        part = dot(swap[...], part).astype(BF16)
        for q in range(QUARTERS):
            x_mat[pl.ds(g * span, span), q * quarter : (q + 1) * quarter] = part[q * span : (q + 1) * span]
        return 0

    lax.fori_loop(0, groups, order_rows, 0)

    for d in range(nx):
        hand_over(d).wait_recv()

    tile = min(256, hidden)
    for t in range(hidden // tile):
        at = t * tile
        gate_w = jnp.concatenate([full_w[j, at : at + tile] for j in range(nx * CORES)], axis=1)
        pre_gate = dot(x_mat[...], gate_w, ((1,), (1,)))
        at += hidden
        up_w = jnp.concatenate([full_w[j, at : at + tile] for j in range(nx * CORES)], axis=1)
        pre_up = dot(x_mat[...], up_w, ((1,), (1,)))
        at -= hidden
        s = jax.nn.sigmoid(pre_gate)
        upstream = cot_mat[:, at : at + tile].astype(F32)
        grad_up = upstream * pre_gate * s
        grad_gate = upstream * pre_up * s * (1.0 + pre_gate * (1.0 - s))
        pair[:, at : at + tile] = grad_gate.astype(BF16)
        pair[:, hidden + at : hidden + at + tile] = grad_up.astype(BF16)
        pair_t[at : at + tile, :] = grad_gate.T.astype(BF16)
        pair_t[hidden + at : hidden + at + tile, :] = grad_up.T.astype(BF16)

    per_quarter = nx * CORES // QUARTERS
    for q in range(QUARTERS):
        parts = [dot(pair[...], full_w[q * per_quarter + i]) for i in range(per_quarter)]
        part = jnp.concatenate(parts, axis=1).astype(BF16)
        for g in range(groups):
            rows_r[g * GROUP + q] = part[g * span : (g + 1) * span]

    left(W, w_r.at[:, pl.ds(0, n - 1)])
    left(COTS, cots_s.at[pl.ds(0, n - 1)])
    left(ROWS, rows_s.at[pl.ds(0, n - 3)])

    def order_back(g, _):
        part = rows_r[pl.ds(g * GROUP, GROUP)].reshape(GROUP * block, quarter)
        part = dot(swap[...], part).astype(BF16)
        rows_s[pl.ds(g * GROUP, GROUP)] = part.reshape(GROUP, block, quarter)
        return 0

    lax.fori_loop(0, groups, order_back, 0)

    def send_back(kind, first, count, sign):
        def start(g, i):
            at_y = lax.rem(y + i, ny)
            pltpu.make_async_remote_copy(
                src_ref=rows_s.at[at_y * nz + plane(-sign * (g + min(first, 1)))],
                dst_ref=back_r.at[(first + g) * ny + y],
                send_sem=send.at[kind],
                recv_sem=recv.at[kind],
                device_id=(dp, at_y * nz + plane(-sign * g)),
                device_id_type=MESH,
            ).start()
            return 0

        lax.fori_loop(ny, count * ny, lambda i, _: start(i // ny, i % ny), 0)
        lax.fori_loop(1, ny, lambda i, _: start(0, i), 0)
        pltpu.make_async_copy(
            rows_s.at[y * nz + plane(-sign * min(first, 1))],
            back_r.at[first * ny + y],
            recv.at[kind],
        ).start()

    sides = ((1, far, side), (1 + far, short, -side))
    send_back(LONG, *sides[0])
    send_back(SHORT, *sides[1])
    send_back(OWN, 0, 1, 0)
    spread_states(LATE)

    chunk = min(384, 2 * hidden)

    def weight_grad(k):
        at = pl.multiple_of(k * CORES * cols, CORES * cols)

        def rows_of(r, _):
            spot = pl.ds(pl.multiple_of(r * chunk, chunk), chunk)
            part = dot(pair_t[spot, :], x_mat[:, pl.ds(at, CORES * cols)]).astype(BF16)
            for i in range(CORES):
                grads[k * CORES + i, spot, :] = part[:, i * cols : (i + 1) * cols]
            return 0

        lax.fori_loop(0, 2 * hidden // chunk, rows_of, 0)

    def halve(d):
        return pltpu.make_async_remote_copy(
            src_ref=grads.at[lax.rem(x + d, nx) * CORES + 1 - core],
            dst_ref=half_r.at[d - 1],
            send_sem=half_send.at[d - 1],
            recv_sem=half_recv.at[d - 1],
            device_id=(twin, me),
            device_id_type=MESH,
        )

    def pass_on(d):
        return pltpu.make_async_remote_copy(
            src_ref=grads.at[x_peer(d)],
            dst_ref=quarter_r.at[d - 1],
            send_sem=sum_send.at[d - 1],
            recv_sem=sum_recv.at[d - 1],
            device_id=(x_peer(d), me),
            device_id_type=MESH,
        )

    for d in range(1, nx + 1):
        weight_grad(lax.rem(x + d, nx))
        halve(d).start()
    for d in range(1, nx + 1):
        halve(d).wait_recv()
        if d < nx:

            def add(r, _):
                spot = pl.ds(pl.multiple_of(r * chunk, chunk), chunk)
                both = grads[x_peer(d), spot, :].astype(F32) + half_r[d - 1, spot, :].astype(F32)
                grads[x_peer(d), spot, :] = both.astype(BF16)
                return 0

            lax.fori_loop(0, 2 * hidden // chunk, add, 0)
            pass_on(d).start()

    def sums(first, count, picks, out):
        for q in range(QUARTERS):
            part = back_r[first * ny : (first + count) * ny].reshape(count * ny * block, quarter)
            out(slice(q * quarter, (q + 1) * quarter), dot(picks[q], part))

    def bring(i, spot=slice(None)):
        return pltpu.make_async_remote_copy(
            src_ref=near_tokens.at[i, :, spot],
            dst_ref=near_back.at[i, :, spot],
            send_sem=bring_send.at[i],
            recv_sem=bring_recv.at[i],
            device_id=(dp, y * nz + plane(-sides[i][2])),
            device_id_type=MESH,
        )

    for i, kind in enumerate((LONG, SHORT)):
        first, count, sign = sides[i]

        def keep(spot, total, i=i):
            near_tokens[i, :, spot] = total.astype(BF16)
            bring(i, pl.ds(spot.start, quarter)).start()

        arrived(kind, back_r.at[pl.ds(first * ny, count * ny)])
        sums(first, count, picks_of[i], keep)

    def keep_own(spot, total):
        own_sum[:, spot] = total

    arrived(OWN, back_r.at[pl.ds(0, ny)])
    sums(0, 1, picks_own, keep_own)

    for d in range(1, nx):
        pass_on(d).wait_recv()
    for i, (moment, a) in enumerate(STATES):
        arrived(STATE + i, moments[moment][1].at[a])

    rows = GROUP * per_source

    def adam(i, _):
        for a in range(2):
            spot = pl.ds(a * hidden + i * rows, rows)
            total = grads[dp, spot, :].astype(F32) + half_r[nx - 1, spot, :].astype(F32)
            for d in range(nx - 1):
                total += quarter_r[d, spot, :].astype(F32)
            gradient = total * (1.0 / loss_scale)
            first = m1_r[a, pl.ds(i * GROUP, GROUP)].astype(F32).reshape(rows, cols)
            second = m2_r[a, pl.ds(i * GROUP, GROUP)].astype(F32).reshape(rows, cols)
            first = beta_one * first + (1.0 - beta_one) * gradient
            second = beta_two * second + (1.0 - beta_two) * gradient * gradient
            weight = full_w[dp, spot, :].astype(F32)
            weight = weight - step_size * first / (jnp.sqrt(second) + adam_eps)
            out = pl.ds(i * rows, rows)
            w_out[a, out, :] = weight.astype(BF16)
            m1_out[a, out, :] = first.astype(BF16)
            m2_out[a, out, :] = second.astype(BF16)
        return 0

    lax.fori_loop(0, groups, adam, 0)

    for i in range(2):
        bring(i).wait_recv()
    token_out[...] = (own_sum[...] + near_back[0].astype(F32) + near_back[1].astype(F32)).astype(BF16)

    for i in range(2):
        for copy in lent(i):
            copy.wait_send()
    for d in range(1, nx):
        gather(d).wait_send()
        pass_on(d).wait_send()
    for d in range(nx):
        hand_over(d).wait_send()
        halve(d + 1).wait_send()
    for i, (moment, a) in enumerate(STATES):
        left(STATE + i, moments[moment][1].at[a, pl.ds(0, n - 1)])
    left(LONG, rows_s.at[pl.ds(0, far * ny - 1)])
    left(SHORT, rows_s.at[pl.ds(0, short * ny - 1)])
    left(OWN, rows_s.at[pl.ds(0, ny - 1)])
    for i in range(2):
        bring(i).wait_send()


def place(*refs):
    count = (len(refs) - 1) // 2
    copies = []
    for i in range(count):
        half = refs[i].shape[0] // 2
        for j in range(2):
            part = pl.ds(j * half, half)
            copies.append(
                pltpu.make_async_copy(refs[i].at[part], refs[count + i].at[part], refs[-1].at[2 * i + j])
            )
    for copy in copies:
        copy.start()
    for copy in copies:
        copy.wait()


def per_device(
    mesh_sizes, tokens, routes, router_gates, hidden_cotangent, weights, first_moment, second_moment
):
    ndp, n = mesh_sizes
    nx = ndp // CORES
    nz = ALONG_Z
    ny = n // nz
    tok, width = tokens.shape
    hidden = hidden_cotangent.shape[2]
    cap = 3 * tok * 2 // (2 * n)
    per_source, cols = weights.shape[2], weights.shape[3]
    block, cot_block, slots = QUARTERS * cap, HALVES * cap, n * cap
    plane = ny * block
    vmem = pl.BlockSpec(memory_space=pltpu.VMEM)
    hbm = pl.BlockSpec(memory_space=pl.ANY)
    shapes = [(tok, width)] + [(2, hidden, cols)] * 3
    dma = pltpu.SemaphoreType.DMA
    results = pl.pallas_call(
        functools.partial(kernel, nx, ny, nz, cap),
        out_shape=tuple(pltpu.VMEM(shape, BF16) for shape in shapes),
        in_specs=[vmem] * 2 + [hbm] * 5,
        out_specs=(vmem,) * 4,
        scratch_shapes=[
            pltpu.VMEM((n, block, width // QUARTERS), BF16),
            pltpu.VMEM((n, block, width // QUARTERS), BF16),
            pltpu.VMEM((n, cot_block, hidden // HALVES), BF16),
            pltpu.VMEM((n, cot_block, hidden // HALVES), BF16),
            pltpu.VMEM((tok, width), BF16),
            pltpu.VMEM((tok, 2, hidden), BF16),
            pltpu.VMEM((tok, 2 * hidden), BF16),
            pltpu.VMEM((2, n, per_source, cols), BF16),
            pltpu.VMEM((2, n, per_source, cols), BF16),
            pltpu.VMEM((2, n, per_source, cols), BF16),
            pltpu.VMEM((ndp, 2 * hidden, cols), BF16),
            pltpu.VMEM((slots, width), BF16),
            pltpu.VMEM((slots, hidden), BF16),
            pltpu.VMEM((slots, 2 * hidden), BF16),
            pltpu.VMEM((2 * hidden, slots), BF16),
            pltpu.VMEM((n, block, width // QUARTERS), BF16),
            pltpu.VMEM((ndp, 2 * hidden, cols), BF16),
            pltpu.VMEM((nx, 2 * hidden, cols), BF16),
            pltpu.VMEM((nx - 1, 2 * hidden, cols), BF16),
            pltpu.VMEM((GROUP * block,) * 2, BF16),
            pltpu.VMEM((GROUP * cot_block,) * 2, BF16),
            pltpu.VMEM((2, tok, width), BF16),
            pltpu.VMEM((2, 2, tok), jnp.int32),
            pltpu.VMEM((2, tok, width), BF16),
            pltpu.VMEM((QUARTERS, tok, plane), BF16),
            pltpu.VMEM((QUARTERS, tok, nz // 2 * plane), BF16),
            pltpu.VMEM((QUARTERS, tok, (nz - 1 - nz // 2) * plane), BF16),
            pltpu.VMEM((tok, width), F32),
            dma((2,)),
            dma((4,)),
            dma((4,)),
            dma((2,)),
            dma((2,)),
            dma((STATE + len(STATES),)),
            dma((STATE + len(STATES),)),
            dma((nx - 1,)),
            dma((nx - 1,)),
            dma((nx,)),
            dma((nx,)),
            dma((nx,)),
            dma((nx,)),
            dma((nx - 1,)),
            dma((nx - 1,)),
        ],
        compiler_params=pltpu.CompilerParams(
            collective_id=0, has_side_effects=True, vmem_limit_bytes=53 * 1024 * 1024
        ),
        name="experts_step",
    )(
        routes.T,
        router_gates.T,
        tokens,
        hidden_cotangent,
        weights,
        first_moment,
        second_moment,
    )
    token_grads, new_w, new_first, new_second = pl.pallas_call(
        place,
        out_shape=tuple(jax.ShapeDtypeStruct(shape, BF16) for shape in shapes),
        in_specs=[vmem] * 4,
        out_specs=(hbm,) * 4,
        scratch_shapes=[dma((8,))],
        compiler_params=pltpu.CompilerParams(vmem_limit_bytes=1024 * 1024),
        name="place",
    )(*(pltpu.with_memory_space_constraint(result, pltpu.VMEM) for result in results))
    shape = (2, 1, hidden, cols)
    return token_grads, new_w.reshape(shape), new_first.reshape(shape), new_second.reshape(shape)


def solution(mesh):
    placed = (
        P(("dp", "expert"), None),
        P(("dp", "expert"), None),
        P(("dp", "expert"), None),
        P(("dp", "expert"), None, None),
        P(None, None, "expert", "dp"),
        P(None, None, "expert", "dp"),
        P(None, None, "expert", "dp"),
    )
    return jax.shard_map(
        functools.partial(per_device, (mesh.shape["dp"], mesh.shape["expert"])),
        mesh=mesh,
        in_specs=placed,
        out_specs=(
            P(("dp", "expert"), None),
            P(None, "expert", None, "dp"),
            P(None, "expert", None, "dp"),
            P(None, "expert", None, "dp"),
        ),
        check_vma=False,
    )
```

```python
import functools

import jax
import jax.numpy as jnp
from jax import lax
from jax.experimental import pallas as pl
from jax.experimental.pallas import tpu as pltpu
from jax.sharding import PartitionSpec as P

gate_unit = 32768.0
loss_scale = 16.0
beta_one = 0.9
beta_two = 0.95
step_size = 0.001
adam_eps = 1e-08

MESH = pl.DeviceIdType.MESH
F32 = jnp.float32
BF16 = jnp.bfloat16
CORES = 2
PIECES = 4
QUARTERS = 4
HALVES = 2
ALONG_Z = 8
GROUP = 4
W, ROWS, COTS, LONG, SHORT, OWN, STATE = range(7)
STATES = ((0, 0), (0, 1), (1, 0), (1, 1))
EARLY, MIDDLE, LATE = (), (0, 1, 2), (3,)


def dot(a, b, dims=((1,), (0,))):
    return lax.dot_general(a, b, (dims, ((), ())), preferred_element_type=F32)


def order_matrix(outer, inner, cap):
    size = outer * inner * cap
    row = lax.broadcasted_iota(jnp.int32, (size, size), 0)
    source = lax.broadcasted_iota(jnp.int32, (size, size), 1)
    a = sum((row >= i * inner * cap).astype(jnp.int32) for i in range(1, outer))
    rest = row - a * (inner * cap)
    b = sum((rest >= i * cap).astype(jnp.int32) for i in range(1, inner))
    return (source == b * (outer * cap) + a * cap + rest - b * cap).astype(BF16)


def kernel(
    nx,
    ny,
    nz,
    cap,
    routes,
    gates,
    tokens_hbm,
    cotangent_hbm,
    w,
    m1,
    m2,
    token_out,
    w_out,
    m1_out,
    m2_out,
    rows_s,
    rows_r,
    cots_s,
    cots_r,
    tokens,
    cotangent,
    scaled,
    w_r,
    m1_r,
    m2_r,
    full_w,
    x_mat,
    cot_mat,
    pair,
    pair_t,
    back_r,
    grads,
    half_r,
    quarter_r,
    swap,
    fold,
    near_tokens,
    near_routes,
    near_back,
    picks_own,
    picks_far,
    picks_short,
    own_sum,
    load_sem,
    near_send,
    near_recv,
    bring_send,
    bring_recv,
    send,
    recv,
    gather_send,
    gather_recv,
    twin_send,
    twin_recv,
    half_send,
    half_recv,
    sum_send,
    sum_recv,
):
    n = ny * nz
    dp, me = lax.axis_index("dp"), lax.axis_index("expert")
    x, core = dp // CORES, dp % CORES
    y, z = me // nz, me % nz
    twin = x * CORES + 1 - core
    tok, width = tokens.shape
    hidden = cotangent.shape[2]
    quarter, half = width // QUARTERS, hidden // HALVES
    per_source, cols = w.shape[2], w.shape[3]
    block = QUARTERS * cap
    cot_block = HALVES * cap
    groups = n // GROUP
    span = GROUP * cap
    slots = n * cap

    def peer(i):
        step = i // ny
        dz = jnp.where(step % 2 == 1, (step + 1) // 2, nz - step // 2)
        return lax.rem(y + i % ny, ny) * nz + lax.rem(z + dz, nz)

    def x_peer(d):
        return lax.rem(x + d, nx) * CORES + core

    loads = [
        pltpu.make_async_copy(source, landing, load_sem.at[i])
        for i, (source, landing) in enumerate(((tokens_hbm, tokens), (cotangent_hbm, cotangent)))
    ]
    for load in loads:
        load.start()

    barrier = pltpu.get_barrier_semaphore()

    def greet(i, _):
        pl.semaphore_signal(barrier, inc=1, device_id=(dp, peer(i)), device_id_type=MESH)
        return 0

    lax.fori_loop(1, n, greet, 0)
    for d in range(1, nx):
        pl.semaphore_signal(barrier, inc=1, device_id=(x_peer(d), me), device_id_type=MESH)
    pl.semaphore_signal(barrier, inc=1, device_id=(twin, me), device_id_type=MESH)
    pl.semaphore_wait(barrier, n - 1 + nx - 1 + 1)

    def spread(kind, source, landing, parts=((ny, n), (1, ny))):
        def start(i, _):
            to = peer(i)
            pltpu.make_async_remote_copy(
                src_ref=source(to),
                dst_ref=landing(me),
                send_sem=send.at[kind],
                recv_sem=recv.at[kind],
                device_id=(dp, to),
                device_id_type=MESH,
            ).start()
            return 0

        for first, last in parts:
            lax.fori_loop(first, last, start, 0)
        pltpu.make_async_copy(source(me), landing(me), recv.at[kind]).start()

    def arrived(kind, ref):
        pltpu.make_async_copy(ref, ref, recv.at[kind]).wait()

    def left(kind, ref):
        pltpu.make_async_copy(ref, ref, send.at[kind]).wait()

    spread(W, lambda e: w.at[:, e], lambda s: w_r.at[:, s])

    side = 1 - 2 * core
    far = nz // 2
    short = nz - 1 - far

    def plane(step):
        return lax.rem(z + step + 2 * nz, nz)

    def lend(source, landing, kind, i):
        return pltpu.make_async_remote_copy(
            src_ref=source,
            dst_ref=landing,
            send_sem=near_send.at[2 * kind + i],
            recv_sem=near_recv.at[2 * kind + i],
            device_id=(dp, y * nz + plane(side * (1 - 2 * i))),
            device_id_type=MESH,
        )

    def lent(i):
        return [
            lend(tokens_hbm, near_tokens.at[i], 0, i),
            lend(routes, near_routes.at[i], 1, i),
        ]

    piece_rows = tok // PIECES
    for i in range(2):
        for j in range(PIECES):
            rows = pl.ds(j * piece_rows, piece_rows)
            lend(tokens_hbm.at[rows], near_tokens.at[i, rows], 0, i).start()
        lend(routes, near_routes.at[i], 1, i).start()
    picks_of = (picks_far, picks_short)

    experts = n
    earlier = lax.broadcasted_iota(jnp.int32, (tok, tok), 0)
    later = lax.broadcasted_iota(jnp.int32, (tok, tok), 1)
    ids = lax.broadcasted_iota(jnp.int32, (experts, tok), 0)

    def number(ref):
        rows = [ref[k : k + 1, :] for k in range(2)]
        hot = [(ids == r).astype(F32) for r in rows]
        before = dot((hot[0] + hot[1]).astype(BF16), (earlier < later).astype(BF16))
        return rows, [jnp.sum(h * before, axis=0, keepdims=True).astype(jnp.int32) for h in hot]

    route_rows, pos_row = number(routes)
    for load in loads:
        load.wait()

    def column(row):
        return jnp.sum(jnp.where(earlier == later, row, jnp.zeros_like(row)), axis=1, keepdims=True)

    for k in range(2):
        factor = column(gates[k : k + 1, :].astype(F32)) * (1.0 / gate_unit)
        scaled[:, k * hidden : (k + 1) * hidden] = (factor * cotangent[:, k, :].astype(F32)).astype(BF16)

    swap[...] = order_matrix(QUARTERS, GROUP, cap)
    fold[...] = order_matrix(HALVES, GROUP, cap)

    piece = lax.broadcasted_iota(jnp.int32, (ny * block, tok), 0)
    cot_piece = lax.broadcasted_iota(jnp.int32, (GROUP * cot_block, tok), 0)

    def pack_cots(g, _):
        first = g * (GROUP * cot_block)
        total = jnp.zeros((GROUP * cot_block, half), F32)
        for k in range(2):
            for h in range(HALVES):
                spot = route_rows[k] * cot_block + pos_row[k] + h * cap - first
                pick = (cot_piece == spot).astype(BF16)
                start = k * hidden + h * half
                total += dot(pick, scaled[:, start : start + half])
        cots_s[pl.ds(g * GROUP, GROUP)] = total.reshape(GROUP, cot_block, half).astype(BF16)
        return 0

    def pack_rows(first, count, sign, numbers, rows, picks):
        places = []
        for k, (r, p) in enumerate(zip(*numbers)):
            at_y = sum((r >= i * nz).astype(jnp.int32) for i in range(1, ny))
            places.append((r - at_y * nz, at_y * block + p))
        spots = []
        for at_z, at in places:
            step = sign * (at_z - z)
            step = jnp.where(step < 0, step + nz, step)
            spots.append(column(jnp.where(step < count, step * (ny * block) + at, -nz * ny * block)))
        position = lax.broadcasted_iota(jnp.int32, (tok, count * ny * block), 1)
        for q in range(QUARTERS):
            pick = (position == spots[0] + q * cap) | (position == spots[1] + q * cap)
            picks[q] = pick.astype(BF16)

        def pack(g, _):
            goal = plane(sign * g)
            total = jnp.zeros((ny * block, quarter), F32)
            for q in range(QUARTERS):
                spot = [jnp.where(at_z == goal, at + q * cap, -1) for at_z, at in places]
                pick = (piece == spot[0]) | (piece == spot[1])
                total += dot(pick.astype(BF16), rows[:, q * quarter : (q + 1) * quarter])
            rows_s[pl.ds((first + g) * ny, ny)] = total.astype(BF16).reshape(ny, block, quarter)
            return 0

        lax.fori_loop(0, count, pack, 0)

    def send_rows(first, count, sign, source_z):
        source = y * nz + source_z

        def start(g, i):
            at_y = lax.rem(y + i, ny)
            pltpu.make_async_remote_copy(
                src_ref=rows_s.at[(first + g) * ny + at_y],
                dst_ref=rows_r.at[source],
                send_sem=send.at[ROWS],
                recv_sem=recv.at[ROWS],
                device_id=(dp, at_y * nz + plane(sign * g)),
                device_id_type=MESH,
            ).start()
            return 0

        lax.fori_loop(ny, count * ny, lambda i, _: start(i // ny, i % ny), 0)
        lax.fori_loop(1, ny, lambda i, _: start(0, i), 0)
        pltpu.make_async_copy(rows_s.at[first * ny + y], rows_r.at[source], recv.at[ROWS]).start()

    lax.fori_loop(0, groups, pack_cots, 0)
    spread(COTS, lambda e: cots_s.at[e], lambda s: cots_r.at[s])
    moments = ((m1, m1_r), (m2, m2_r))

    def spread_states(which):
        for i in which:
            moment, a = STATES[i]
            source, landing = moments[moment]
            spread(
                STATE + i,
                lambda e, source=source, a=a: source.at[a, e],
                lambda s, landing=landing, a=a: landing.at[a, s],
            )

    spread_states(EARLY)
    pack_rows(0, 1, 1, (route_rows, pos_row), tokens, picks_own)
    send_rows(0, 1, 0, z)
    arrived(W, w_r)

    def own_columns(i, _):
        for a in range(2):
            part = w_r[a, pl.ds(i * GROUP, GROUP)].astype(F32)
            rows = GROUP * per_source
            full_w[dp, pl.ds(a * hidden + i * rows, rows), :] = part.reshape(rows, cols).astype(BF16)
        return 0

    lax.fori_loop(0, groups, own_columns, 0)

    def gather(d):
        return pltpu.make_async_remote_copy(
            src_ref=full_w.at[dp],
            dst_ref=full_w.at[dp],
            send_sem=gather_send.at[d - 1],
            recv_sem=gather_recv.at[d - 1],
            device_id=(x_peer(d), me),
            device_id_type=MESH,
        )

    def hand_over(d):
        held = lax.rem(x - d + nx, nx) * CORES + core
        return pltpu.make_async_remote_copy(
            src_ref=full_w.at[held],
            dst_ref=full_w.at[held],
            send_sem=twin_send.at[d],
            recv_sem=twin_recv.at[d],
            device_id=(twin, me),
            device_id_type=MESH,
        )

    for d in range(1, nx):
        gather(d).start()
    hand_over(0).start()

    for i, (first, count, sign) in enumerate(((1, far, side), (1 + far, short, -side))):
        for copy in lent(i):
            copy.wait_recv()
        pack_rows(first, count, sign, number(near_routes.at[i]), near_tokens.at[i], picks_of[i])
        send_rows(first, count, sign, plane(-sign))
    spread_states(MIDDLE)

    for d in range(1, nx):
        gather(d).wait_recv()
        hand_over(d).start()

    arrived(COTS, cots_r)

    def order_cots(g, _):
        part = cots_r[pl.ds(g * GROUP, GROUP)].astype(F32).reshape(GROUP * cot_block, half)
        part = dot(fold[...], part.astype(BF16)).astype(BF16)
        for h in range(HALVES):
            cot_mat[pl.ds(g * span, span), h * half : (h + 1) * half] = part[h * span : (h + 1) * span]
        return 0

    lax.fori_loop(0, groups, order_cots, 0)
    arrived(ROWS, rows_r)

    def order_rows(g, _):
        part = rows_r[pl.ds(g * GROUP, GROUP)].reshape(GROUP * block, quarter)
        part = dot(swap[...], part).astype(BF16)
        for q in range(QUARTERS):
            x_mat[pl.ds(g * span, span), q * quarter : (q + 1) * quarter] = part[q * span : (q + 1) * span]
        return 0

    lax.fori_loop(0, groups, order_rows, 0)

    for d in range(nx):
        hand_over(d).wait_recv()

    tile = min(256, hidden)
    for t in range(hidden // tile):
        at = t * tile
        gate_w = jnp.concatenate([full_w[j, at : at + tile] for j in range(nx * CORES)], axis=1)
        pre_gate = dot(x_mat[...], gate_w, ((1,), (1,)))
        at += hidden
        up_w = jnp.concatenate([full_w[j, at : at + tile] for j in range(nx * CORES)], axis=1)
        pre_up = dot(x_mat[...], up_w, ((1,), (1,)))
        at -= hidden
        s = jax.nn.sigmoid(pre_gate)
        upstream = cot_mat[:, at : at + tile].astype(F32)
        grad_up = upstream * pre_gate * s
        grad_gate = upstream * pre_up * s * (1.0 + pre_gate * (1.0 - s))
        pair[:, at : at + tile] = grad_gate.astype(BF16)
        pair[:, hidden + at : hidden + at + tile] = grad_up.astype(BF16)
        pair_t[at : at + tile, :] = grad_gate.T.astype(BF16)
        pair_t[hidden + at : hidden + at + tile, :] = grad_up.T.astype(BF16)

    per_quarter = nx * CORES // QUARTERS
    for q in range(QUARTERS):
        parts = [dot(pair[...], full_w[q * per_quarter + i]) for i in range(per_quarter)]
        part = jnp.concatenate(parts, axis=1).astype(BF16)
        for g in range(groups):
            rows_r[g * GROUP + q] = part[g * span : (g + 1) * span]

    left(W, w_r.at[:, pl.ds(0, n - 1)])
    left(COTS, cots_s.at[pl.ds(0, n - 1)])
    left(ROWS, rows_s.at[pl.ds(0, n - 3)])

    def order_back(g, _):
        part = rows_r[pl.ds(g * GROUP, GROUP)].reshape(GROUP * block, quarter)
        part = dot(swap[...], part).astype(BF16)
        rows_s[pl.ds(g * GROUP, GROUP)] = part.reshape(GROUP, block, quarter)
        return 0

    lax.fori_loop(0, groups, order_back, 0)

    def send_back(kind, first, count, sign):
        def start(g, i):
            at_y = lax.rem(y + i, ny)
            pltpu.make_async_remote_copy(
                src_ref=rows_s.at[at_y * nz + plane(-sign * (g + min(first, 1)))],
                dst_ref=back_r.at[(first + g) * ny + y],
                send_sem=send.at[kind],
                recv_sem=recv.at[kind],
                device_id=(dp, at_y * nz + plane(-sign * g)),
                device_id_type=MESH,
            ).start()
            return 0

        lax.fori_loop(ny, count * ny, lambda i, _: start(i // ny, i % ny), 0)
        lax.fori_loop(1, ny, lambda i, _: start(0, i), 0)
        pltpu.make_async_copy(
            rows_s.at[y * nz + plane(-sign * min(first, 1))],
            back_r.at[first * ny + y],
            recv.at[kind],
        ).start()

    sides = ((1, far, side), (1 + far, short, -side))
    send_back(LONG, *sides[0])
    send_back(SHORT, *sides[1])
    send_back(OWN, 0, 1, 0)
    spread_states(LATE)

    chunk = min(384, 2 * hidden)

    def weight_grad(k):
        at = pl.multiple_of(k * CORES * cols, CORES * cols)

        def rows_of(r, _):
            spot = pl.ds(pl.multiple_of(r * chunk, chunk), chunk)
            part = dot(pair_t[spot, :], x_mat[:, pl.ds(at, CORES * cols)]).astype(BF16)
            for i in range(CORES):
                grads[k * CORES + i, spot, :] = part[:, i * cols : (i + 1) * cols]
            return 0

        lax.fori_loop(0, 2 * hidden // chunk, rows_of, 0)

    def halve(d):
        return pltpu.make_async_remote_copy(
            src_ref=grads.at[lax.rem(x + d, nx) * CORES + 1 - core],
            dst_ref=half_r.at[d - 1],
            send_sem=half_send.at[d - 1],
            recv_sem=half_recv.at[d - 1],
            device_id=(twin, me),
            device_id_type=MESH,
        )

    def pass_on(d):
        return pltpu.make_async_remote_copy(
            src_ref=grads.at[x_peer(d)],
            dst_ref=quarter_r.at[d - 1],
            send_sem=sum_send.at[d - 1],
            recv_sem=sum_recv.at[d - 1],
            device_id=(x_peer(d), me),
            device_id_type=MESH,
        )

    for d in range(1, nx + 1):
        weight_grad(lax.rem(x + d, nx))
        halve(d).start()
    for d in range(1, nx + 1):
        halve(d).wait_recv()
        if d < nx:

            def add(r, _):
                spot = pl.ds(pl.multiple_of(r * chunk, chunk), chunk)
                both = grads[x_peer(d), spot, :].astype(F32) + half_r[d - 1, spot, :].astype(F32)
                grads[x_peer(d), spot, :] = both.astype(BF16)
                return 0

            lax.fori_loop(0, 2 * hidden // chunk, add, 0)
            pass_on(d).start()

    def sums(first, count, picks, out):
        for q in range(QUARTERS):
            part = back_r[first * ny : (first + count) * ny].reshape(count * ny * block, quarter)
            out(slice(q * quarter, (q + 1) * quarter), dot(picks[q], part))

    def bring(i, q):
        spot = pl.ds(q * quarter, quarter)
        return pltpu.make_async_remote_copy(
            src_ref=near_tokens.at[i, :, spot],
            dst_ref=near_back.at[i, :, spot],
            send_sem=bring_send.at[i, q],
            recv_sem=bring_recv.at[i, q],
            device_id=(dp, y * nz + plane(-sides[i][2])),
            device_id_type=MESH,
        )

    for i, kind in enumerate((LONG, SHORT)):
        first, count, sign = sides[i]

        def keep(spot, total, i=i):
            near_tokens[i, :, spot] = total.astype(BF16)
            bring(i, spot.start // quarter).start()

        arrived(kind, back_r.at[pl.ds(first * ny, count * ny)])
        sums(first, count, picks_of[i], keep)

    def keep_own(spot, total):
        own_sum[:, spot] = total

    arrived(OWN, back_r.at[pl.ds(0, ny)])
    sums(0, 1, picks_own, keep_own)

    for d in range(1, nx):
        pass_on(d).wait_recv()
    for i, (moment, a) in enumerate(STATES):
        arrived(STATE + i, moments[moment][1].at[a])

    rows = GROUP * per_source

    def adam(i, _):
        for a in range(2):
            spot = pl.ds(a * hidden + i * rows, rows)
            total = grads[dp, spot, :].astype(F32) + half_r[nx - 1, spot, :].astype(F32)
            for d in range(nx - 1):
                total += quarter_r[d, spot, :].astype(F32)
            gradient = total * (1.0 / loss_scale)
            first = m1_r[a, pl.ds(i * GROUP, GROUP)].astype(F32).reshape(rows, cols)
            second = m2_r[a, pl.ds(i * GROUP, GROUP)].astype(F32).reshape(rows, cols)
            first = beta_one * first + (1.0 - beta_one) * gradient
            second = beta_two * second + (1.0 - beta_two) * gradient * gradient
            weight = full_w[dp, spot, :].astype(F32)
            weight = weight - step_size * first / (jnp.sqrt(second) + adam_eps)
            out = pl.ds(i * rows, rows)
            w_out[a, out, :] = weight.astype(BF16)
            m1_out[a, out, :] = first.astype(BF16)
            m2_out[a, out, :] = second.astype(BF16)
        return 0

    lax.fori_loop(0, groups, adam, 0)

    for q in range(QUARTERS):
        spot = slice(q * quarter, (q + 1) * quarter)
        total = own_sum[:, spot]
        for i in range(2):
            bring(i, q).wait_recv()
            total += near_back[i, :, spot].astype(F32)
        token_out[:, spot] = total.astype(BF16)

    for i in range(2):
        for copy in lent(i):
            copy.wait_send()
    for d in range(1, nx):
        gather(d).wait_send()
        pass_on(d).wait_send()
    for d in range(nx):
        hand_over(d).wait_send()
        halve(d + 1).wait_send()
    for i, (moment, a) in enumerate(STATES):
        left(STATE + i, moments[moment][1].at[a, pl.ds(0, n - 1)])
    left(LONG, rows_s.at[pl.ds(0, far * ny - 1)])
    left(SHORT, rows_s.at[pl.ds(0, short * ny - 1)])
    left(OWN, rows_s.at[pl.ds(0, ny - 1)])
    for i in range(2):
        for q in range(QUARTERS):
            bring(i, q).wait_send()


def place(*refs):
    count = (len(refs) - 1) // 2
    copies = []
    for i in range(count):
        half = refs[i].shape[0] // 2
        for j in range(2):
            part = pl.ds(j * half, half)
            copies.append(
                pltpu.make_async_copy(refs[i].at[part], refs[count + i].at[part], refs[-1].at[2 * i + j])
            )
    for copy in copies:
        copy.start()
    for copy in copies:
        copy.wait()


def per_device(
    mesh_sizes, tokens, routes, router_gates, hidden_cotangent, weights, first_moment, second_moment
):
    ndp, n = mesh_sizes
    nx = ndp // CORES
    nz = ALONG_Z
    ny = n // nz
    tok, width = tokens.shape
    hidden = hidden_cotangent.shape[2]
    cap = 3 * tok * 2 // (2 * n)
    per_source, cols = weights.shape[2], weights.shape[3]
    block, cot_block, slots = QUARTERS * cap, HALVES * cap, n * cap
    plane = ny * block
    vmem = pl.BlockSpec(memory_space=pltpu.VMEM)
    hbm = pl.BlockSpec(memory_space=pl.ANY)
    shapes = [(tok, width)] + [(2, hidden, cols)] * 3
    dma = pltpu.SemaphoreType.DMA
    results = pl.pallas_call(
        functools.partial(kernel, nx, ny, nz, cap),
        out_shape=tuple(pltpu.VMEM(shape, BF16) for shape in shapes),
        in_specs=[vmem] * 2 + [hbm] * 5,
        out_specs=(vmem,) * 4,
        scratch_shapes=[
            pltpu.VMEM((n, block, width // QUARTERS), BF16),
            pltpu.VMEM((n, block, width // QUARTERS), BF16),
            pltpu.VMEM((n, cot_block, hidden // HALVES), BF16),
            pltpu.VMEM((n, cot_block, hidden // HALVES), BF16),
            pltpu.VMEM((tok, width), BF16),
            pltpu.VMEM((tok, 2, hidden), BF16),
            pltpu.VMEM((tok, 2 * hidden), BF16),
            pltpu.VMEM((2, n, per_source, cols), BF16),
            pltpu.VMEM((2, n, per_source, cols), BF16),
            pltpu.VMEM((2, n, per_source, cols), BF16),
            pltpu.VMEM((ndp, 2 * hidden, cols), BF16),
            pltpu.VMEM((slots, width), BF16),
            pltpu.VMEM((slots, hidden), BF16),
            pltpu.VMEM((slots, 2 * hidden), BF16),
            pltpu.VMEM((2 * hidden, slots), BF16),
            pltpu.VMEM((n, block, width // QUARTERS), BF16),
            pltpu.VMEM((ndp, 2 * hidden, cols), BF16),
            pltpu.VMEM((nx, 2 * hidden, cols), BF16),
            pltpu.VMEM((nx - 1, 2 * hidden, cols), BF16),
            pltpu.VMEM((GROUP * block,) * 2, BF16),
            pltpu.VMEM((GROUP * cot_block,) * 2, BF16),
            pltpu.VMEM((2, tok, width), BF16),
            pltpu.VMEM((2, 2, tok), jnp.int32),
            pltpu.VMEM((2, tok, width), BF16),
            pltpu.VMEM((QUARTERS, tok, plane), BF16),
            pltpu.VMEM((QUARTERS, tok, nz // 2 * plane), BF16),
            pltpu.VMEM((QUARTERS, tok, (nz - 1 - nz // 2) * plane), BF16),
            pltpu.VMEM((tok, width), F32),
            dma((2,)),
            dma((4,)),
            dma((4,)),
            dma((2, QUARTERS)),
            dma((2, QUARTERS)),
            dma((STATE + len(STATES),)),
            dma((STATE + len(STATES),)),
            dma((nx - 1,)),
            dma((nx - 1,)),
            dma((nx,)),
            dma((nx,)),
            dma((nx,)),
            dma((nx,)),
            dma((nx - 1,)),
            dma((nx - 1,)),
        ],
        compiler_params=pltpu.CompilerParams(
            collective_id=0, has_side_effects=True, vmem_limit_bytes=53 * 1024 * 1024
        ),
        name="experts_step",
    )(
        routes.T,
        router_gates.T,
        tokens,
        hidden_cotangent,
        weights,
        first_moment,
        second_moment,
    )
    token_grads, new_w, new_first, new_second = pl.pallas_call(
        place,
        out_shape=tuple(jax.ShapeDtypeStruct(shape, BF16) for shape in shapes),
        in_specs=[vmem] * 4,
        out_specs=(hbm,) * 4,
        scratch_shapes=[dma((8,))],
        compiler_params=pltpu.CompilerParams(vmem_limit_bytes=1024 * 1024),
        name="place",
    )(*(pltpu.with_memory_space_constraint(result, pltpu.VMEM) for result in results))
    shape = (2, 1, hidden, cols)
    return token_grads, new_w.reshape(shape), new_first.reshape(shape), new_second.reshape(shape)


def solution(mesh):
    placed = (
        P(("dp", "expert"), None),
        P(("dp", "expert"), None),
        P(("dp", "expert"), None),
        P(("dp", "expert"), None, None),
        P(None, None, "expert", "dp"),
        P(None, None, "expert", "dp"),
        P(None, None, "expert", "dp"),
    )
    return jax.shard_map(
        functools.partial(per_device, (mesh.shape["dp"], mesh.shape["expert"])),
        mesh=mesh,
        in_specs=placed,
        out_specs=(
            P(("dp", "expert"), None),
            P(None, "expert", None, "dp"),
            P(None, "expert", None, "dp"),
            P(None, "expert", None, "dp"),
        ),
        check_vma=False,
    )
```
